32 devices in a mesh: cells: 8 (over y, x, core), snap: 4 (over z).
Axes of the slice: x: 2, y: 2, z: 4, core: 2. Of those that a mesh axis runs over, the one named last changes fastest.
Arguments:
- snapshots: bfloat16 [3, 8192, 1024], P(None, 'cells', 'snap'), may hold values from -10 to 10
- mass_blocks: bfloat16 [128, 64, 64], P('cells'), may hold values from -0.25 to 4.25
- block_offsets: int32 [128], P('cells'), may hold values from 0 to 8128, as said below
Outputs:
- gram: float32 [1024, 1024], P('snap', 'cells')
The draws below stay inside these ranges and needn't reach their ends.
Inputs may be any that keep to these rules, and one draw needn't show every extreme that they name: `block_offsets`: offsets are multiples of 64; the blocks of the g-th aligned group of 16 blocks start at distinct offsets that together cover cells g * 1024 to (g + 1) * 1024 - 1.
All inputs are finite; a program needn't handle non-finite values.
Results may differ from the reference program's by a relative error of at most 0.0003.
Values may be sent and summed in bfloat16 or wider, within the bound.
No kernel may reach another device: no remote copies, remote signals or barrier semaphores. Data moves between devices by JAX's collectives and lax.ppermute only.
A program may use at most 128 MiB of HBM per device.

```python
import jax
import jax.numpy as jnp
from jax import lax

COMPS = 3
BLOCK = 64
CELL_DEV = 1024
CELLS = 8192
SNAPS = 1024
BLOCKS = 128


def draw_snapshots(key, part):
    key = jax.random.fold_in(key, 11)
    first, second, third = jax.random.split(key, 3)
    common = 0.6 * jax.random.truncated_normal(first, -3.0, 3.0, (1, CELLS, 1), jnp.float32) * jax.random.truncated_normal(second, -3.0, 3.0, (1, 1, SNAPS), jnp.float32)
    noise = jax.random.truncated_normal(third, -4.0, 4.0, (COMPS, CELLS, SNAPS), jnp.float32)
    return (common + noise).astype(jnp.bfloat16)


def draw_mass_blocks(key, part):
    key = jax.random.fold_in(key, 23)
    first, second = jax.random.split(key, 2)
    diagonal = jax.random.uniform(first, (BLOCKS, BLOCK), jnp.float32, 2.0, 4.0)
    noise = 0.08 * jax.random.truncated_normal(second, -3.0, 3.0, (BLOCKS, BLOCK, BLOCK), jnp.float32)
    identity = jnp.eye(BLOCK, dtype=jnp.float32)
    result = noise * (1.0 - identity)[None] + diagonal[:, :, None] * identity[None]
    return result.astype(jnp.bfloat16)


def draw_block_offsets(key, part):
    key = jax.random.fold_in(key, 37)
    block_count = CELL_DEV // BLOCK
    group_count = BLOCKS // block_count
    groups = jnp.arange(group_count, dtype=jnp.int32)
    orders = jax.vmap(lambda group: jax.random.permutation(jax.random.fold_in(key, group), block_count))(groups)
    starts = groups[:, None] * block_count + orders.astype(jnp.int32)
    return (starts * BLOCK).reshape(-1).astype(jnp.int32)


def setup_inputs(seed: int = 0) -> dict:
    key_of = jax.random.split(jax.random.key(seed), 4)
    snapshots = draw_snapshots(jax.random.fold_in(key_of[3], 71), 0)
    mass_blocks = draw_mass_blocks(jax.random.fold_in(key_of[3], 71), 0)
    block_offsets = draw_block_offsets(jax.random.fold_in(key_of[3], 71), 0)
    return {"snapshots": snapshots, "mass_blocks": mass_blocks, "block_offsets": block_offsets}


def reference(snapshots, mass_blocks, block_offsets):
    block_count = CELL_DEV // BLOCK
    group_count = BLOCKS // block_count
    within = jnp.arange(BLOCK, dtype=jnp.int32)

    def stepper(accum, group):
        offsets_now = lax.dynamic_slice_in_dim(block_offsets, group * block_count, block_count)
        masses_now = lax.dynamic_slice_in_dim(mass_blocks, group * block_count, block_count)
        row_index = (offsets_now[:, None] + within[None, :]).reshape(-1).astype(jnp.int32)
        selected = jnp.take(snapshots, row_index, axis=1).reshape(COMPS, block_count, BLOCK, SNAPS)
        weighted = jnp.einsum("bij,cbjs->cbis", masses_now.astype(jnp.float32), selected.astype(jnp.float32)).astype(jnp.bfloat16)
        left_rows = selected.reshape(COMPS * block_count * BLOCK, SNAPS)
        right_rows = weighted.reshape(COMPS * block_count * BLOCK, SNAPS)
        return accum + jnp.dot(left_rows.T, right_rows, preferred_element_type=jnp.float32), None

    groups = jnp.arange(group_count, dtype=jnp.int32)
    total, _ = lax.scan(stepper, jnp.zeros((SNAPS, SNAPS), jnp.float32), groups)
    return total * (1.0 / float(3 * CELLS))
```

```python
import functools

import jax
import jax.numpy as jnp
from jax import lax
from jax.experimental import pallas as pl
from jax.experimental.pallas import tpu as pltpu
from jax.sharding import PartitionSpec as P

BF16, F32 = jnp.bfloat16, jnp.float32


def general(snapshots, mass_blocks, block_offsets):
    components, cell_rows, columns_dev = snapshots.shape
    blocks_dev = mass_blocks.shape[0]
    block_size = mass_blocks.shape[1]
    base_block = lax.axis_index("cells") * blocks_dev
    local_index = block_offsets // block_size - base_block
    selected = jnp.take(
        snapshots.reshape(components, blocks_dev, block_size, columns_dev), local_index, axis=1
    )
    weighted = jnp.einsum(
        "bij,cbjs->cbis", mass_blocks, selected, preferred_element_type=F32
    ).astype(BF16)
    left_rows = selected.reshape(components * cell_rows, columns_dev)
    right_rows = weighted.reshape(components * cell_rows, columns_dev)
    product = lax.dot_general(
        left_rows,
        lax.all_gather(right_rows, "snap", axis=1, tiled=True),
        (((0,), (0,)), ((), ())),
        preferred_element_type=F32,
    )
    factor = 1.0 / float(3 * cell_rows * lax.axis_size("cells"))
    result = lax.psum_scatter(product, "cells", scatter_dimension=1, tiled=True)
    return result * factor


STAGE_C = ((0, 0), (2, 0), (2, 1), (0, 2), (1, 2))
START_C = (0, 2, 3, 3)
STAGE_D = ((1, 0), (3, 0), (0, 1), (3, 1), (0, 3), (1, 3))
START_D = (0, 2, 4, 4)


def tdot(left, right):
    return lax.dot_general(left, right, (((0,), (0,)), ((), ())), preferred_element_type=F32)


def weigh(diagonal, piece):
    return jnp.concatenate(
        [
            jnp.dot(diagonal, piece[c], preferred_element_type=F32).astype(BF16)
            for c in range(piece.shape[0])
        ],
        axis=0,
    )


def flat(piece):
    return piece.reshape(piece.shape[0] * piece.shape[1], piece.shape[2])


def put(core, block, own_ref, other_ref, at):
    half = block.shape[1] // 2
    low, high = block[:, :half], block[:, half:]
    first = core == 0
    own_ref[at] = jnp.where(first, low, high)
    other_ref[at] = jnp.where(first, high, low)


def early_kernel(offsets_ref, mass_ref, s_ref, diagonal_ref, weighted_ref, gram_ref, where_ref):
    components, cell_rows, _ = s_ref.shape
    blocks, size, _ = mass_ref.shape
    quarters, rows, _ = diagonal_ref.shape
    base = lax.axis_index("cells") * blocks
    for b in range(blocks):
        where_ref[offsets_ref[b] // size - base] = b
    diagonal_ref[...] = jnp.zeros_like(diagonal_ref)
    per = blocks // quarters
    for t in range(quarters):
        for i in range(per):
            diagonal_ref[t, i * size : (i + 1) * size, i * size : (i + 1) * size] = mass_ref[
                where_ref[t * per + i]
            ]
    for t in range(quarters):
        for c in range(components):
            rows_now = slice(t * rows, (t + 1) * rows)
            weighted_ref[c, rows_now, :] = jnp.dot(
                diagonal_ref[t], s_ref[c, rows_now, :], preferred_element_type=F32
            ).astype(BF16)
    total = tdot(s_ref[0], weighted_ref[0])
    for c in range(1, components):
        total += tdot(s_ref[c], weighted_ref[c])
    gram_ref[...] = total


def stage_c_kernel(
    scale, s_ref, weighted_ref, diagonal_ref, gram_ref, s1_ref, s2_ref, own_ref, other_ref
):
    z, core = lax.axis_index("snap"), lax.axis_index("cells") % 2
    rows = s2_ref.shape[1]
    mine = pl.ds(pl.multiple_of(z * rows, rows), rows)
    diagonal = diagonal_ref[z]
    s0, w0 = flat(s_ref[:, mine, :]), flat(weighted_ref[:, mine, :])
    s1, s2 = flat(s1_ref[...]), flat(s2_ref[...])
    w1, w2 = weigh(diagonal, s1_ref[...]), weigh(diagonal, s2_ref[...])
    blocks = {
        (0, 0): lambda: gram_ref[...],
        (2, 0): lambda: tdot(s2, w0),
        (2, 1): lambda: tdot(s2, w1),
        (0, 2): lambda: tdot(s0, w2),
        (1, 2): lambda: tdot(s1, w2),
    }
    for at, name in enumerate(STAGE_C):
        put(core, blocks[name]() * scale, own_ref, other_ref, at)


def stage_d_kernel(
    scale, s_ref, weighted_ref, diagonal_ref, s1_ref, s1b_ref, s3_ref, own_ref, other_ref
):
    z, core = lax.axis_index("snap"), lax.axis_index("cells") % 2
    rows = s3_ref.shape[1]
    across = z ^ 2
    mine = pl.ds(pl.multiple_of(z * rows, rows), rows)
    more = pl.ds(pl.multiple_of(across * rows, rows), rows)
    diagonal = diagonal_ref[z]
    s0, w0 = flat(s_ref[:, mine, :]), flat(weighted_ref[:, mine, :])
    s0b, w0b = flat(s_ref[:, more, :]), flat(weighted_ref[:, more, :])
    s1, s1b, s3 = flat(s1_ref[...]), flat(s1b_ref[...]), flat(s3_ref[...])
    w1, w3 = weigh(diagonal, s1_ref[...]), weigh(diagonal, s3_ref[...])
    w1b = weigh(diagonal_ref[across], s1b_ref[...])
    blocks = {
        (1, 0): lambda: tdot(s1, w0) + tdot(s1b, w0b),
        (3, 0): lambda: tdot(s3, w0),
        (0, 1): lambda: tdot(s0, w1) + tdot(s0b, w1b),
        (3, 1): lambda: tdot(s3, w1),
        (0, 3): lambda: tdot(s0, w3),
        (1, 3): lambda: tdot(s1, w3),
    }
    for at, name in enumerate(STAGE_D):
        put(core, blocks[name]() * scale, own_ref, other_ref, at)


def call(kernel, outs, flops, name, *args, smem=(), scratch=()):
    vmem, scalar = pl.BlockSpec(memory_space=pltpu.VMEM), pl.BlockSpec(memory_space=pltpu.SMEM)
    return pl.pallas_call(
        kernel,
        out_shape=[jax.ShapeDtypeStruct(s, t) for s, t in outs],
        in_specs=[scalar if k in smem else vmem for k in range(len(args))],
        out_specs=[vmem] * len(outs),
        scratch_shapes=scratch,
        compiler_params=pltpu.CompilerParams(vmem_limit_bytes=40 * 2**20),
        cost_estimate=pl.CostEstimate(flops=flops, bytes_accessed=4 * 2**20, transcendentals=0),
        name=name,
    )(*args)


def fast(snapshots, mass_blocks, block_offsets):
    components, cell_rows, columns = snapshots.shape
    planes, devices = lax.axis_size("snap"), lax.axis_size("cells")
    rows, half = cell_rows // planes, columns // 2
    scale = 1.0 / float(components * cell_rows * devices)
    z, cells = lax.axis_index("snap"), lax.axis_index("cells")
    q = (cells // 2) ^ z

    def to_plane(array, m):
        return lax.ppermute(array, "snap", [(i, i ^ m) for i in range(planes)])

    def rows_of(m):
        return lax.dynamic_slice_in_dim(snapshots, (z ^ m) * rows, rows, axis=1)

    def send(array, m, k, wanted):
        pairs = []
        for c in range(devices):
            for i in range(planes):
                to_c, to_i = c ^ (2 * m), i ^ k
                if ((to_c // 2) ^ to_i) in wanted:
                    pairs.append((c * planes + i, to_c * planes + to_i))
        return lax.ppermute(array, ("cells", "snap"), pairs)

    out2, out1, out3 = rows_of(2), rows_of(1), rows_of(3)
    s2 = to_plane(out2, 2)
    s1 = to_plane(out1, 1)
    s3 = to_plane(out3, 3)
    s1b = to_plane(out3, 1)

    diagonal, weighted, gram = call(
        early_kernel,
        [((planes, rows, rows), BF16), (snapshots.shape, BF16), ((columns, columns), F32)],
        2 * 2 * components * cell_rows * columns * columns,
        "early",
        block_offsets,
        mass_blocks,
        snapshots,
        smem=(0,),
        scratch=[pltpu.SMEM((mass_blocks.shape[0],), jnp.int32)],
    )

    def reduced(own, other, starts, wanted):
        arrived = lax.ppermute(other, "cells", [(c, c ^ 1) for c in range(devices)])

        def window(to):
            start = jnp.asarray(starts, jnp.int32)[to]
            return lax.dynamic_slice_in_dim(own, start, 2, 0) + lax.dynamic_slice_in_dim(
                arrived, start, 2, 0
            )

        total = window(q)
        for m in (1, 2, 3):
            total += send(window(q ^ m), m, 0, wanted)
        return total

    def stage(kernel, blocks, name, *args):
        shape = (len(blocks), columns, half)
        return call(
            functools.partial(kernel, scale),
            [(shape, F32), (shape, F32)],
            2 * len(blocks) * components * rows * columns * columns,
            name,
            *args,
        )

    own, other = stage(
        stage_c_kernel, STAGE_C, "stage_c", snapshots, weighted, diagonal, gram, s1, s2
    )
    sum_c = reduced(own, other, START_C, (0, 1, 2))
    from2 = send(jnp.where(q == 0, sum_c[1], sum_c[0]), 0, 2, (2, 3))
    own, other = stage(
        stage_d_kernel, STAGE_D, "stage_d", snapshots, weighted, diagonal, s1, s1b, s3
    )
    sum_d = reduced(own, other, START_D, (0, 1, 3))
    keep = jnp.where(q % 2 == 0, sum_c[0], sum_d[0])
    keep = jnp.where(q == 2, sum_c[0], keep)
    one = jnp.where(q == 0, sum_d[0], jnp.where(q == 2, sum_c[1], sum_d[1]))
    from1 = send(one, 0, 1, (1, 2, 3))
    from3 = send(sum_d[1], 0, 3, (2, 3))
    return keep + from1 + from2 + from3


def solution(mesh):
    fits = mesh.shape["cells"] == 8 and mesh.shape["snap"] == 4
    placed = (P(None, "cells", "snap"), P("cells", None, None), P("cells"))
    return jax.shard_map(
        fast if fits else general,
        mesh=mesh,
        in_specs=placed,
        out_specs=P("snap", "cells"),
        check_vma=False,
    )
```

```python
import functools

import jax
import jax.numpy as jnp
from jax import lax
from jax.experimental import pallas as pl
from jax.experimental.pallas import tpu as pltpu
from jax.sharding import PartitionSpec as P

BF16, F32 = jnp.bfloat16, jnp.float32


def general(snapshots, mass_blocks, block_offsets):
    components, cell_rows, columns_dev = snapshots.shape
    blocks_dev = mass_blocks.shape[0]
    block_size = mass_blocks.shape[1]
    base_block = lax.axis_index("cells") * blocks_dev
    local_index = block_offsets // block_size - base_block
    selected = jnp.take(
        snapshots.reshape(components, blocks_dev, block_size, columns_dev), local_index, axis=1
    )
    weighted = jnp.einsum(
        "bij,cbjs->cbis", mass_blocks, selected, preferred_element_type=F32
    ).astype(BF16)
    left_rows = selected.reshape(components * cell_rows, columns_dev)
    right_rows = weighted.reshape(components * cell_rows, columns_dev)
    product = lax.dot_general(
        left_rows,
        lax.all_gather(right_rows, "snap", axis=1, tiled=True),
        (((0,), (0,)), ((), ())),
        preferred_element_type=F32,
    )
    factor = 1.0 / float(3 * cell_rows * lax.axis_size("cells"))
    result = lax.psum_scatter(product, "cells", scatter_dimension=1, tiled=True)
    return result * factor


STAGE_C = ((0, 0), (2, 0), (2, 1), (0, 2), (1, 2))
START_C = (0, 2, 3, 3)
STAGE_D = ((1, 0), (3, 0), (0, 1), (3, 1), (0, 3), (1, 3))
START_D = (0, 2, 4, 4)


def tdot(left, right):
    return lax.dot_general(left, right, (((0,), (0,)), ((), ())), preferred_element_type=F32)


def weigh(diagonal, piece):
    return jnp.concatenate(
        [
            jnp.dot(diagonal, piece[c], preferred_element_type=F32).astype(BF16)
            for c in range(piece.shape[0])
        ],
        axis=0,
    )


def flat(piece):
    return piece.reshape(piece.shape[0] * piece.shape[1], piece.shape[2])


def put(core, block, own_ref, other_ref, at):
    half = block.shape[1] // 2
    low, high = block[:, :half], block[:, half:]
    first = core == 0
    own_ref[at] = jnp.where(first, low, high)
    other_ref[at] = jnp.where(first, high, low)


def early_kernel(offsets_ref, mass_ref, s_ref, diagonal_ref, weighted_ref, gram_ref, where_ref):
    components, cell_rows, _ = s_ref.shape
    blocks, size, _ = mass_ref.shape
    quarters, rows, _ = diagonal_ref.shape
    base = lax.axis_index("cells") * blocks
    for b in range(blocks):
        where_ref[offsets_ref[b] // size - base] = b
    diagonal_ref[...] = jnp.zeros_like(diagonal_ref)
    per = blocks // quarters
    for t in range(quarters):
        for i in range(per):
            diagonal_ref[t, i * size : (i + 1) * size, i * size : (i + 1) * size] = mass_ref[
                where_ref[t * per + i]
            ]
    for t in range(quarters):
        for c in range(components):
            rows_now = slice(t * rows, (t + 1) * rows)
            weighted_ref[c, rows_now, :] = jnp.dot(
                diagonal_ref[t], s_ref[c, rows_now, :], preferred_element_type=F32
            ).astype(BF16)
    total = tdot(s_ref[0], weighted_ref[0])
    for c in range(1, components):
        total += tdot(s_ref[c], weighted_ref[c])
    gram_ref[...] = total


def stage_c_kernel(
    scale, s_ref, weighted_ref, diagonal_ref, gram_ref, s1_ref, s2_ref, own_ref, other_ref
):
    z, core = lax.axis_index("snap"), lax.axis_index("cells") % 2
    rows = s2_ref.shape[1]
    mine = pl.ds(pl.multiple_of(z * rows, rows), rows)
    diagonal = diagonal_ref[z]
    s0, w0 = flat(s_ref[:, mine, :]), flat(weighted_ref[:, mine, :])
    s1, s2 = flat(s1_ref[...]), flat(s2_ref[...])
    w1, w2 = weigh(diagonal, s1_ref[...]), weigh(diagonal, s2_ref[...])
    blocks = {
        (0, 0): lambda: gram_ref[...],
        (2, 0): lambda: tdot(s2, w0),
        (2, 1): lambda: tdot(s2, w1),
        (0, 2): lambda: tdot(s0, w2),
        (1, 2): lambda: tdot(s1, w2),
    }
    for at, name in enumerate(STAGE_C):
        put(core, blocks[name]() * scale, own_ref, other_ref, at)


def stage_d_kernel(
    scale, s_ref, weighted_ref, diagonal_ref, s1_ref, s1b_ref, s3_ref, own_ref, other_ref
):
    z, core = lax.axis_index("snap"), lax.axis_index("cells") % 2
    rows = s3_ref.shape[1]
    across = z ^ 2
    mine = pl.ds(pl.multiple_of(z * rows, rows), rows)
    more = pl.ds(pl.multiple_of(across * rows, rows), rows)
    diagonal = diagonal_ref[z]
    s0, w0 = flat(s_ref[:, mine, :]), flat(weighted_ref[:, mine, :])
    s0b, w0b = flat(s_ref[:, more, :]), flat(weighted_ref[:, more, :])
    s1, s1b, s3 = flat(s1_ref[...]), flat(s1b_ref[...]), flat(s3_ref[...])
    w1, w3 = weigh(diagonal, s1_ref[...]), weigh(diagonal, s3_ref[...])
    w1b = weigh(diagonal_ref[across], s1b_ref[...])
    blocks = {
        (1, 0): lambda: tdot(s1, w0) + tdot(s1b, w0b),
        (3, 0): lambda: tdot(s3, w0),
        (0, 1): lambda: tdot(s0, w1) + tdot(s0b, w1b),
        (3, 1): lambda: tdot(s3, w1),
        (0, 3): lambda: tdot(s0, w3),
        (1, 3): lambda: tdot(s1, w3),
    }
    for at, name in enumerate(STAGE_D):
        put(core, blocks[name]() * scale, own_ref, other_ref, at)


GROUP = 64
TAIL = 16
STEPS = 256.0
TOP = 32700.0


def encode(value, message_ref):
    slots, rows, columns = value.shape
    groups = slots * rows // GROUP
    value = value.reshape(groups, GROUP, columns)
    most = jnp.maximum(jnp.max(jnp.abs(value), axis=1), 1e-36)
    step = jnp.ceil(jnp.log2(most) * STEPS)
    code = jnp.round(value * (TOP * jnp.exp2(step * (-1.0 / STEPS)))[:, None, :])
    codes = code.reshape(slots * rows, columns).astype(jnp.int32).astype(jnp.int16)
    message_ref[: slots * rows] = codes
    step = jnp.concatenate([step, jnp.zeros((TAIL - groups, columns), F32)], axis=0)
    message_ref[slots * rows :] = step.astype(jnp.int32).astype(jnp.int16)


def decode(message_ref, slots):
    total, columns = message_ref.shape
    rows = (total - TAIL) // slots
    groups = slots * rows // GROUP
    step = message_ref[slots * rows :].astype(jnp.int32).astype(F32)[:groups]
    code = message_ref[: slots * rows].astype(jnp.int32).astype(F32)
    value = code.reshape(groups, GROUP, columns) * (jnp.exp2(step * (1.0 / STEPS)) * (1.0 / TOP))[:, None, :]
    return value.reshape(slots, rows, columns)


def place():
    return (lax.axis_index("cells") // 2) ^ lax.axis_index("snap")


def combine_kernel(starts, own_ref, arrived_ref, total_ref, *message_refs):
    q = place()
    for m, ref in enumerate((total_ref, *message_refs)):
        to = q ^ m
        start = jnp.where(
            to == 0, starts[0], jnp.where(to == 1, starts[1], jnp.where(to == 2, starts[2], starts[3]))
        )
        value = own_ref[pl.ds(start, 2)] + arrived_ref[pl.ds(start, 2)]
        if m == 0:
            ref[...] = value
        else:
            encode(value, ref)


def plane_sum(total_ref, message_refs):
    total = total_ref[...]
    for ref in message_refs:
        total += decode(ref, 2)
    return total


def plane_c_kernel(total_ref, m1_ref, m2_ref, m3_ref, sum_ref, two_ref):
    total = plane_sum(total_ref, (m1_ref, m2_ref, m3_ref))
    sum_ref[...] = total
    encode(jnp.where(place() == 0, total[1:], total[:1]), two_ref)


def plane_d_kernel(total_ref, m1_ref, m2_ref, m3_ref, sum_c_ref, keep_ref, one_ref, three_ref):
    q = place()
    total = plane_sum(total_ref, (m1_ref, m2_ref, m3_ref))
    encode(jnp.where(q == 0, total[:1], jnp.where(q == 2, sum_c_ref[1:], total[1:])), one_ref)
    encode(total[1:], three_ref)
    keep_ref[...] = jnp.where(q % 2 == 0, sum_c_ref[0], total[0])


def last_kernel(keep_ref, m1_ref, m2_ref, m3_ref, out_ref):
    out_ref[...] = (
        keep_ref[...] + decode(m1_ref, 1)[0] + decode(m2_ref, 1)[0] + decode(m3_ref, 1)[0]
    )


def call(kernel, outs, flops, name, *args, smem=(), scratch=()):
    vmem, scalar = pl.BlockSpec(memory_space=pltpu.VMEM), pl.BlockSpec(memory_space=pltpu.SMEM)
    return pl.pallas_call(
        kernel,
        out_shape=[jax.ShapeDtypeStruct(s, t) for s, t in outs],
        in_specs=[scalar if k in smem else vmem for k in range(len(args))],
        out_specs=[vmem] * len(outs),
        scratch_shapes=scratch,
        compiler_params=pltpu.CompilerParams(vmem_limit_bytes=LIMIT),
        cost_estimate=pl.CostEstimate(flops=flops, bytes_accessed=2**20, transcendentals=0),
        name=name,
    )(*args)


LIMIT = 24 * 2**20


def fast(snapshots, mass_blocks, block_offsets):
    components, cell_rows, columns = snapshots.shape
    planes, devices = lax.axis_size("snap"), lax.axis_size("cells")
    rows, half = cell_rows // planes, columns // 2
    scale = 1.0 / float(components * cell_rows * devices)
    z = lax.axis_index("snap")

    def to_plane(array, m):
        return lax.ppermute(array, "snap", [(i, i ^ m) for i in range(planes)])

    def rows_of(array, m):
        return lax.dynamic_slice_in_dim(array, (z ^ m) * rows, rows, axis=1)

    def send(array, m, k, wanted):
        pairs = []
        for c in range(devices):
            for i in range(planes):
                to_c, to_i = c ^ (2 * m), i ^ k
                if ((to_c // 2) ^ to_i) in wanted:
                    pairs.append((c * planes + i, to_c * planes + to_i))
        return lax.ppermute(array, ("cells", "snap"), pairs)

    out2 = rows_of(snapshots, 2)
    later, _ = lax.optimization_barrier((snapshots, out2))
    out1 = rows_of(later, 1)
    out3 = rows_of(later, 3)
    s2 = to_plane(out2, 2)
    s1 = to_plane(out1, 1)
    s3 = to_plane(out3, 3)
    s1b = to_plane(out3, 1)

    diagonal, weighted, gram = call(
        early_kernel,
        [((planes, rows, rows), BF16), (snapshots.shape, BF16), ((columns, columns), F32)],
        2 * 2 * components * cell_rows * columns * columns,
        "early",
        block_offsets,
        mass_blocks,
        later,
        smem=(0,),
        scratch=[pltpu.SMEM((mass_blocks.shape[0],), jnp.int32)],
    )

    pair, single = ((2 * columns + TAIL, half), jnp.int16), ((columns + TAIL, half), jnp.int16)

    def plane(own, other, starts, wanted, name):
        arrived = lax.ppermute(other, "cells", [(c, c ^ 1) for c in range(devices)])
        total, *out = call(
            functools.partial(combine_kernel, starts),
            [((2, columns, half), F32), pair, pair, pair],
            0,
            name,
            own,
            arrived,
        )
        return total, [send(out[m - 1], m, 0, wanted) for m in (1, 2, 3)]

    def stage(kernel, blocks, name, *args):
        shape = (len(blocks), columns, half)
        return call(
            functools.partial(kernel, scale),
            [(shape, F32), (shape, F32)],
            2 * len(blocks) * components * rows * columns * columns,
            name,
            *args,
        )

    own, other = stage(
        stage_c_kernel, STAGE_C, "stage_c", snapshots, weighted, diagonal, gram, s1, s2
    )
    total, arrived = plane(own, other, START_C, (0, 1, 2), "combine_c")
    sum_c, two = call(
        plane_c_kernel, [((2, columns, half), F32), single], 0, "plane_c", total, *arrived
    )
    from2 = send(two, 0, 2, (2, 3))
    s1b, s3, sum_c = lax.optimization_barrier((s1b, s3, sum_c))
    own, other = stage(
        stage_d_kernel, STAGE_D, "stage_d", snapshots, weighted, diagonal, s1, s1b, s3
    )
    total, arrived = plane(own, other, START_D, (0, 1, 3), "combine_d")
    keep, one, three = call(
        plane_d_kernel, [((columns, half), F32), single, single], 0, "plane_d", total, *arrived, sum_c
    )
    from1 = send(one, 0, 1, (1, 2, 3))
    from3 = send(three, 0, 3, (2, 3))
    return call(last_kernel, [((columns, half), F32)], 0, "last", keep, from1, from2, from3)[0]


def solution(mesh):
    fits = mesh.shape["cells"] == 8 and mesh.shape["snap"] == 4
    placed = (P(None, "cells", "snap"), P("cells", None, None), P("cells"))
    return jax.shard_map(
        fast if fits else general,
        mesh=mesh,
        in_specs=placed,
        out_specs=P("snap", "cells"),
        check_vma=False,
    )
```

```python
import functools

import jax
import jax.numpy as jnp
from jax import lax
from jax.experimental import pallas as pl
from jax.experimental.pallas import tpu as pltpu
from jax.sharding import PartitionSpec as P

BF16, F32 = jnp.bfloat16, jnp.float32


def general(snapshots, mass_blocks, block_offsets):
    components, cell_rows, columns_dev = snapshots.shape
    blocks_dev = mass_blocks.shape[0]
    block_size = mass_blocks.shape[1]
    base_block = lax.axis_index("cells") * blocks_dev
    local_index = block_offsets // block_size - base_block
    selected = jnp.take(
        snapshots.reshape(components, blocks_dev, block_size, columns_dev), local_index, axis=1
    )
    weighted = jnp.einsum(
        "bij,cbjs->cbis", mass_blocks, selected, preferred_element_type=F32
    ).astype(BF16)
    left_rows = selected.reshape(components * cell_rows, columns_dev)
    right_rows = weighted.reshape(components * cell_rows, columns_dev)
    product = lax.dot_general(
        left_rows,
        lax.all_gather(right_rows, "snap", axis=1, tiled=True),
        (((0,), (0,)), ((), ())),
        preferred_element_type=F32,
    )
    factor = 1.0 / float(3 * cell_rows * lax.axis_size("cells"))
    result = lax.psum_scatter(product, "cells", scatter_dimension=1, tiled=True)
    return result * factor


STAGE_C = ((0, 0), (2, 0), (2, 1), (0, 2), (1, 2))
START_C = (0, 2, 3, 3)
STAGE_D = ((1, 0), (3, 0), (0, 1), (3, 1), (0, 3), (1, 3))
START_D = (0, 2, 4, 4)


def tdot(left, right):
    return lax.dot_general(left, right, (((0,), (0,)), ((), ())), preferred_element_type=F32)


def weigh(diagonal, piece):
    return jnp.concatenate(
        [
            jnp.dot(diagonal, piece[c], preferred_element_type=F32).astype(BF16)
            for c in range(piece.shape[0])
        ],
        axis=0,
    )


def flat(piece):
    return piece.reshape(piece.shape[0] * piece.shape[1], piece.shape[2])


def put(core, block, own_ref, other_ref, at):
    half = block.shape[1] // 2
    low, high = block[:, :half], block[:, half:]
    first = core == 0
    own_ref[at] = jnp.where(first, low, high)
    other_ref[at] = jnp.where(first, high, low)


def early_kernel(offsets_ref, mass_ref, s_ref, diagonal_ref, weighted_ref, gram_ref, where_ref):
    components, cell_rows, _ = s_ref.shape
    blocks, size, _ = mass_ref.shape
    quarters, rows, _ = diagonal_ref.shape
    base = lax.axis_index("cells") * blocks
    for b in range(blocks):
        where_ref[offsets_ref[b] // size - base] = b
    diagonal_ref[...] = jnp.zeros_like(diagonal_ref)
    per = blocks // quarters
    for t in range(quarters):
        for i in range(per):
            diagonal_ref[t, i * size : (i + 1) * size, i * size : (i + 1) * size] = mass_ref[
                where_ref[t * per + i]
            ]
    for t in range(quarters):
        for c in range(components):
            rows_now = slice(t * rows, (t + 1) * rows)
            weighted_ref[c, rows_now, :] = jnp.dot(
                diagonal_ref[t], s_ref[c, rows_now, :], preferred_element_type=F32
            ).astype(BF16)
    total = tdot(s_ref[0], weighted_ref[0])
    for c in range(1, components):
        total += tdot(s_ref[c], weighted_ref[c])
    gram_ref[...] = total


def stage_c_kernel(
    scale, s_ref, weighted_ref, diagonal_ref, gram_ref, s1_ref, s2_ref, own_ref, other_ref
):
    z, core = lax.axis_index("snap"), lax.axis_index("cells") % 2
    rows = s2_ref.shape[1]
    mine = pl.ds(pl.multiple_of(z * rows, rows), rows)
    diagonal = diagonal_ref[z]
    s0, w0 = flat(s_ref[:, mine, :]), flat(weighted_ref[:, mine, :])
    s1, s2 = flat(s1_ref[...]), flat(s2_ref[...])
    w1, w2 = weigh(diagonal, s1_ref[...]), weigh(diagonal, s2_ref[...])
    blocks = {
        (0, 0): lambda: gram_ref[...],
        (2, 0): lambda: tdot(s2, w0),
        (2, 1): lambda: tdot(s2, w1),
        (0, 2): lambda: tdot(s0, w2),
        (1, 2): lambda: tdot(s1, w2),
    }
    for at, name in enumerate(STAGE_C):
        put(core, blocks[name]() * scale, own_ref, other_ref, at)


def stage_d_kernel(
    scale, s_ref, weighted_ref, diagonal_ref, s1_ref, s1b_ref, s3_ref, own_ref, other_ref
):
    z, core = lax.axis_index("snap"), lax.axis_index("cells") % 2
    rows = s3_ref.shape[1]
    across = z ^ 2
    mine = pl.ds(pl.multiple_of(z * rows, rows), rows)
    more = pl.ds(pl.multiple_of(across * rows, rows), rows)
    diagonal = diagonal_ref[z]
    s0, w0 = flat(s_ref[:, mine, :]), flat(weighted_ref[:, mine, :])
    s0b, w0b = flat(s_ref[:, more, :]), flat(weighted_ref[:, more, :])
    s1, s1b, s3 = flat(s1_ref[...]), flat(s1b_ref[...]), flat(s3_ref[...])
    w1, w3 = weigh(diagonal, s1_ref[...]), weigh(diagonal, s3_ref[...])
    w1b = weigh(diagonal_ref[across], s1b_ref[...])
    blocks = {
        (1, 0): lambda: tdot(s1, w0) + tdot(s1b, w0b),
        (3, 0): lambda: tdot(s3, w0),
        (0, 1): lambda: tdot(s0, w1) + tdot(s0b, w1b),
        (3, 1): lambda: tdot(s3, w1),
        (0, 3): lambda: tdot(s0, w3),
        (1, 3): lambda: tdot(s1, w3),
    }
    for at, name in enumerate(STAGE_D):
        put(core, blocks[name]() * scale, own_ref, other_ref, at)


GROUP = 64
TAIL = 16
STEPS = 256.0
TOP = 32700.0


def encode(value, message_ref):
    slots, rows, columns = value.shape
    groups = slots * rows // GROUP
    value = value.reshape(groups, GROUP, columns)
    most = jnp.maximum(jnp.max(jnp.abs(value), axis=1), 1e-36)
    step = jnp.ceil(jnp.log2(most) * STEPS)
    code = jnp.round(value * (TOP * jnp.exp2(step * (-1.0 / STEPS)))[:, None, :])
    codes = code.reshape(slots * rows, columns).astype(jnp.int32).astype(jnp.int16)
    message_ref[: slots * rows] = codes
    step = jnp.concatenate([step, jnp.zeros((TAIL - groups, columns), F32)], axis=0)
    message_ref[slots * rows :] = step.astype(jnp.int32).astype(jnp.int16)


def decode(message_ref, slots):
    total, columns = message_ref.shape
    rows = (total - TAIL) // slots
    groups = slots * rows // GROUP
    step = message_ref[slots * rows :].astype(jnp.int32).astype(F32)[:groups]
    code = message_ref[: slots * rows].astype(jnp.int32).astype(F32)
    value = code.reshape(groups, GROUP, columns) * (jnp.exp2(step * (1.0 / STEPS)) * (1.0 / TOP))[:, None, :]
    return value.reshape(slots, rows, columns)


def place():
    return (lax.axis_index("cells") // 2) ^ lax.axis_index("snap")


def combine_kernel(starts, own_ref, arrived_ref, total_ref, *message_refs):
    q = place()
    for m, ref in enumerate((total_ref, *message_refs)):
        to = q ^ m
        start = jnp.where(
            to == 0, starts[0], jnp.where(to == 1, starts[1], jnp.where(to == 2, starts[2], starts[3]))
        )
        value = own_ref[pl.ds(start, 2)] + arrived_ref[pl.ds(start, 2)]
        if m == 0:
            ref[...] = value
        else:
            encode(value, ref)


def plane_sum(total_ref, message_refs):
    total = total_ref[...]
    for ref in message_refs:
        total += decode(ref, 2)
    return total


def plane_c_kernel(total_ref, m1_ref, m2_ref, m3_ref, sum_ref, two_ref):
    total = plane_sum(total_ref, (m1_ref, m2_ref, m3_ref))
    sum_ref[...] = total
    encode(jnp.where(place() == 0, total[1:], total[:1]), two_ref)


def plane_d_kernel(total_ref, m1_ref, m2_ref, m3_ref, sum_c_ref, keep_ref, one_ref, three_ref):
    q = place()
    total = plane_sum(total_ref, (m1_ref, m2_ref, m3_ref))
    encode(jnp.where(q == 0, total[:1], jnp.where(q == 2, sum_c_ref[1:], total[1:])), one_ref)
    encode(total[1:], three_ref)
    keep_ref[...] = jnp.where(q % 2 == 0, sum_c_ref[0], total[0])


def last_kernel(keep_ref, m1_ref, m2_ref, m3_ref, out_ref):
    out_ref[...] = (
        keep_ref[...] + decode(m1_ref, 1)[0] + decode(m2_ref, 1)[0] + decode(m3_ref, 1)[0]
    )


def call(kernel, outs, flops, name, *args, smem=(), scratch=()):
    vmem, scalar = pl.BlockSpec(memory_space=pltpu.VMEM), pl.BlockSpec(memory_space=pltpu.SMEM)
    return pl.pallas_call(
        kernel,
        out_shape=[jax.ShapeDtypeStruct(s, t) for s, t in outs],
        in_specs=[scalar if k in smem else vmem for k in range(len(args))],
        out_specs=[vmem] * len(outs),
        scratch_shapes=scratch,
        compiler_params=pltpu.CompilerParams(vmem_limit_bytes=LIMIT),
        cost_estimate=pl.CostEstimate(flops=0, bytes_accessed=0, transcendentals=0),
        name=name,
    )(*args)


LIMIT = 24 * 2**20


def fast(snapshots, mass_blocks, block_offsets):
    components, cell_rows, columns = snapshots.shape
    planes, devices = lax.axis_size("snap"), lax.axis_size("cells")
    rows, half = cell_rows // planes, columns // 2
    scale = 1.0 / float(components * cell_rows * devices)
    z = lax.axis_index("snap")

    def to_plane(array, m):
        return lax.ppermute(array, "snap", [(i, i ^ m) for i in range(planes)])

    def rows_of(array, m):
        return lax.dynamic_slice_in_dim(array, (z ^ m) * rows, rows, axis=1)

    def send(array, m, k, wanted):
        pairs = []
        for c in range(devices):
            for i in range(planes):
                to_c, to_i = c ^ (2 * m), i ^ k
                if ((to_c // 2) ^ to_i) in wanted:
                    pairs.append((c * planes + i, to_c * planes + to_i))
        return lax.ppermute(array, ("cells", "snap"), pairs)

    out2, out1, out3 = rows_of(snapshots, 2), rows_of(snapshots, 1), rows_of(snapshots, 3)
    s2 = to_plane(out2, 2)
    s1 = to_plane(out1, 1)
    s3 = to_plane(out3, 3)
    s1b = to_plane(out3, 1)

    diagonal, weighted, gram = call(
        early_kernel,
        [((planes, rows, rows), BF16), (snapshots.shape, BF16), ((columns, columns), F32)],
        2 * 2 * components * cell_rows * columns * columns,
        "early",
        block_offsets,
        mass_blocks,
        snapshots,
        smem=(0,),
        scratch=[pltpu.SMEM((mass_blocks.shape[0],), jnp.int32)],
    )

    pair, single = ((2 * columns + TAIL, half), jnp.int16), ((columns + TAIL, half), jnp.int16)

    def plane(own, other, starts, wanted, name):
        arrived = lax.ppermute(other, "cells", [(c, c ^ 1) for c in range(devices)])
        total, *out = call(
            functools.partial(combine_kernel, starts),
            [((2, columns, half), F32), pair, pair, pair],
            0,
            name,
            own,
            arrived,
        )
        return total, [send(out[m - 1], m, 0, wanted) for m in (1, 2, 3)]

    def stage(kernel, blocks, name, *args):
        shape = (len(blocks), columns, half)
        return call(
            functools.partial(kernel, scale),
            [(shape, F32), (shape, F32)],
            2 * len(blocks) * components * rows * columns * columns,
            name,
            *args,
        )

    def chain(weighted, diagonal, gram, s1, s2):
        own, other = stage(
            stage_c_kernel, STAGE_C, "stage_c", snapshots, weighted, diagonal, gram, s1, s2
        )
        total, arrived = plane(own, other, START_C, (0, 1, 2), "combine_c")
        return tuple(
            call(plane_c_kernel, [((2, columns, half), F32), single], 0, "plane_c", total, *arrived)
        )

    def never(weighted, diagonal, gram, s1, s2):
        return jnp.zeros((2, columns, half), F32), jnp.zeros(*single)

    sum_c, two = lax.cond(z < planes, chain, never, weighted, diagonal, gram, s1, s2)
    from2 = send(two, 0, 2, (2, 3))
    s1b, s3, sum_c = lax.optimization_barrier((s1b, s3, sum_c))
    own, other = stage(
        stage_d_kernel, STAGE_D, "stage_d", snapshots, weighted, diagonal, s1, s1b, s3
    )
    total, arrived = plane(own, other, START_D, (0, 1, 3), "combine_d")
    keep, one, three = call(
        plane_d_kernel, [((columns, half), F32), single, single], 0, "plane_d", total, *arrived, sum_c
    )
    from1 = send(one, 0, 1, (1, 2, 3))
    from3 = send(three, 0, 3, (2, 3))
    return call(last_kernel, [((columns, half), F32)], 0, "last", keep, from1, from2, from3)[0]


def solution(mesh):
    fits = mesh.shape["cells"] == 8 and mesh.shape["snap"] == 4
    placed = (P(None, "cells", "snap"), P("cells", None, None), P("cells"))
    return jax.shard_map(
        fast if fits else general,
        mesh=mesh,
        in_specs=placed,
        out_specs=P("snap", "cells"),
        check_vma=False,
    )
```

```python
import functools

import jax
import jax.numpy as jnp
from jax import lax
from jax.experimental import pallas as pl
from jax.experimental.pallas import tpu as pltpu
from jax.sharding import PartitionSpec as P

BF16, F32 = jnp.bfloat16, jnp.float32


def general(snapshots, mass_blocks, block_offsets):
    components, cell_rows, columns_dev = snapshots.shape
    blocks_dev = mass_blocks.shape[0]
    block_size = mass_blocks.shape[1]
    base_block = lax.axis_index("cells") * blocks_dev
    local_index = block_offsets // block_size - base_block
    selected = jnp.take(
        snapshots.reshape(components, blocks_dev, block_size, columns_dev), local_index, axis=1
    )
    weighted = jnp.einsum(
        "bij,cbjs->cbis", mass_blocks, selected, preferred_element_type=F32
    ).astype(BF16)
    left_rows = selected.reshape(components * cell_rows, columns_dev)
    right_rows = weighted.reshape(components * cell_rows, columns_dev)
    product = lax.dot_general(
        left_rows,
        lax.all_gather(right_rows, "snap", axis=1, tiled=True),
        (((0,), (0,)), ((), ())),
        preferred_element_type=F32,
    )
    factor = 1.0 / float(3 * cell_rows * lax.axis_size("cells"))
    result = lax.psum_scatter(product, "cells", scatter_dimension=1, tiled=True)
    return result * factor


STAGE_C = ((2, 0), (2, 1), (0, 2))
STAGE_D = ((1, 0), (3, 0), (0, 1), (3, 1), (0, 3), (1, 3), (1, 2))
START_D = (0, 2, 5, 4)


def tdot(left, right):
    return lax.dot_general(left, right, (((0,), (0,)), ((), ())), preferred_element_type=F32)


def weigh(diagonal, piece):
    return jnp.concatenate(
        [
            jnp.dot(diagonal, piece[c], preferred_element_type=F32).astype(BF16)
            for c in range(piece.shape[0])
        ],
        axis=0,
    )


def flat(piece):
    return piece.reshape(piece.shape[0] * piece.shape[1], piece.shape[2])


def halves(core, block):
    half = block.shape[1] // 2
    low, high = block[:, :half], block[:, half:]
    first = core == 0
    return jnp.where(first, low, high), jnp.where(first, high, low)


def early_kernel(
    scale, offsets_ref, mass_ref, s_ref, diagonal_ref, weighted_ref, own_ref, other_ref, where_ref
):
    components = s_ref.shape[0]
    blocks, size, _ = mass_ref.shape
    quarters, rows, _ = diagonal_ref.shape
    cells = lax.axis_index("cells")
    base = cells * blocks
    for b in range(blocks):
        where_ref[offsets_ref[b] // size - base] = b
    diagonal_ref[...] = jnp.zeros_like(diagonal_ref)
    per = blocks // quarters
    for t in range(quarters):
        for i in range(per):
            diagonal_ref[t, i * size : (i + 1) * size, i * size : (i + 1) * size] = mass_ref[
                where_ref[t * per + i]
            ]
    for t in range(quarters):
        for c in range(components):
            rows_now = slice(t * rows, (t + 1) * rows)
            weighted_ref[c, rows_now, :] = jnp.dot(
                diagonal_ref[t], s_ref[c, rows_now, :], preferred_element_type=F32
            ).astype(BF16)
    total = tdot(s_ref[0], weighted_ref[0])
    for c in range(1, components):
        total += tdot(s_ref[c], weighted_ref[c])
    own_ref[...], other_ref[...] = halves(cells % 2, total * scale)


def stage_c_kernel(
    scale, s_ref, weighted_ref, diagonal_ref, s1_ref, s2_ref, own_ref, other_ref, later_ref
):
    z, core = lax.axis_index("snap"), lax.axis_index("cells") % 2
    rows = s2_ref.shape[1]
    mine = pl.ds(pl.multiple_of(z * rows, rows), rows)
    diagonal = diagonal_ref[z]
    s0, w0 = flat(s_ref[:, mine, :]), flat(weighted_ref[:, mine, :])
    s1, s2 = flat(s1_ref[...]), flat(s2_ref[...])
    w1, w2 = weigh(diagonal, s1_ref[...]), weigh(diagonal, s2_ref[...])
    blocks = {(2, 0): tdot(s2, w0), (2, 1): tdot(s2, w1), (0, 2): tdot(s0, w2)}
    others = []
    for at, name in enumerate(STAGE_C):
        own_ref[at], other = halves(core, blocks[name] * scale)
        others.append(other)
    encode(jnp.stack(others), other_ref)
    later_ref[...] = tdot(s1, w2)


def stage_d_kernel(
    scale,
    s_ref,
    weighted_ref,
    diagonal_ref,
    later_ref,
    s1_ref,
    s1b_ref,
    s3_ref,
    own_ref,
    other_ref,
):
    z, core = lax.axis_index("snap"), lax.axis_index("cells") % 2
    rows = s3_ref.shape[1]
    across = z ^ 2
    mine = pl.ds(pl.multiple_of(z * rows, rows), rows)
    more = pl.ds(pl.multiple_of(across * rows, rows), rows)
    diagonal = diagonal_ref[z]
    s0, w0 = flat(s_ref[:, mine, :]), flat(weighted_ref[:, mine, :])
    s0b, w0b = flat(s_ref[:, more, :]), flat(weighted_ref[:, more, :])
    s1, s1b, s3 = flat(s1_ref[...]), flat(s1b_ref[...]), flat(s3_ref[...])
    w1, w3 = weigh(diagonal, s1_ref[...]), weigh(diagonal, s3_ref[...])
    w1b = weigh(diagonal_ref[across], s1b_ref[...])
    blocks = {
        (1, 0): tdot(s1, w0) + tdot(s1b, w0b),
        (3, 0): tdot(s3, w0),
        (0, 1): tdot(s0, w1) + tdot(s0b, w1b),
        (3, 1): tdot(s3, w1),
        (0, 3): tdot(s0, w3),
        (1, 3): tdot(s1, w3),
        (1, 2): later_ref[...],
    }
    others = []
    for at, name in enumerate(STAGE_D):
        own_ref[at], other = halves(core, blocks[name] * scale)
        others.append(other)
    encode(jnp.stack(others), other_ref)


GROUP = 64
TAIL = 32
STEPS = 256.0
TOP = 32700.0


def encode(value, message_ref):
    slots, rows, columns = value.shape
    groups = slots * rows // GROUP
    value = value.reshape(groups, GROUP, columns)
    most = jnp.maximum(jnp.max(jnp.abs(value), axis=1), 1e-36)
    step = jnp.ceil(jnp.log2(most) * STEPS)
    code = jnp.round(value * (TOP * jnp.exp2(step * (-1.0 / STEPS)))[:, None, :])
    codes = code.reshape(slots * rows, columns).astype(jnp.int32).astype(jnp.int16)
    message_ref[: slots * rows] = codes
    step = jnp.concatenate([step, jnp.zeros((TAIL - groups, columns), F32)], axis=0)
    message_ref[slots * rows :] = step.astype(jnp.int32).astype(jnp.int16)


def decode(message_ref, slots):
    total, columns = message_ref.shape
    rows = (total - TAIL) // slots
    groups = slots * rows // GROUP
    step = message_ref[slots * rows :].astype(jnp.int32).astype(F32)[:groups]
    code = message_ref[: slots * rows].astype(jnp.int32).astype(F32)
    value = code.reshape(groups, GROUP, columns) * (jnp.exp2(step * (1.0 / STEPS)) * (1.0 / TOP))[:, None, :]
    return value.reshape(slots, rows, columns)


def place():
    return (lax.axis_index("cells") // 2) ^ lax.axis_index("snap")


def combine_c_kernel(own_ref, arrived_ref, one_ref, other_ref, total_ref, *message_refs):
    q = place()
    whole = own_ref[...] + decode(arrived_ref, len(STAGE_C))
    square = one_ref[...] + other_ref[...]
    for m, ref in enumerate((total_ref, *message_refs)):
        to = q ^ m
        first = jnp.where(to == 0, whole[0], jnp.where(to == 1, whole[1], whole[2]))
        value = jnp.stack([first, square])
        if m == 0:
            ref[...] = value
        else:
            encode(value, ref)


def combine_d_kernel(own_ref, arrived_ref, total_ref, *refs):
    *message_refs, whole_ref = refs
    q = place()
    whole_ref[...] = own_ref[...] + decode(arrived_ref, len(STAGE_D))
    for m, ref in enumerate((total_ref, *message_refs)):
        to = q ^ m
        start = jnp.where(to == 1, START_D[1], jnp.where(to == 2, START_D[2], START_D[3]))
        value = whole_ref[pl.ds(jnp.where(to == 0, START_D[0], start), 2)]
        if m == 0:
            ref[...] = value
        else:
            encode(value, ref)


def plane_sum(total_ref, message_refs):
    total = total_ref[...]
    for ref in message_refs:
        total += decode(ref, 2)
    return total


def plane_c_kernel(total_ref, m1_ref, m2_ref, m3_ref, keep_ref, two_ref):
    total = plane_sum(total_ref, (m1_ref, m2_ref, m3_ref))
    encode(total[:1], two_ref)
    keep_ref[...] = jnp.where(place() == 0, total[1], total[0])


def plane_d_kernel(total_ref, m1_ref, m2_ref, m3_ref, keep_c_ref, keep_ref, one_ref, three_ref):
    q = place()
    total = plane_sum(total_ref, (m1_ref, m2_ref, m3_ref))
    encode(jnp.where(q == 0, total[:1], total[1:]), one_ref)
    encode(total[1:], three_ref)
    keep_ref[...] = jnp.where(q % 2 == 0, keep_c_ref[...], total[0])


def last_kernel(keep_ref, m1_ref, m2_ref, m3_ref, out_ref):
    out_ref[...] = (
        keep_ref[...] + decode(m1_ref, 1)[0] + decode(m2_ref, 1)[0] + decode(m3_ref, 1)[0]
    )


def call(kernel, outs, name, *args, smem=(), scratch=()):
    vmem, scalar = pl.BlockSpec(memory_space=pltpu.VMEM), pl.BlockSpec(memory_space=pltpu.SMEM)
    return pl.pallas_call(
        kernel,
        out_shape=[jax.ShapeDtypeStruct(s, t) for s, t in outs],
        in_specs=[scalar if k in smem else vmem for k in range(len(args))],
        out_specs=[vmem] * len(outs),
        scratch_shapes=scratch,
        compiler_params=pltpu.CompilerParams(vmem_limit_bytes=LIMIT),
        cost_estimate=pl.CostEstimate(flops=0, bytes_accessed=0, transcendentals=0),
        name=name,
    )(*args)


LIMIT = 24 * 2**20


def fast(snapshots, mass_blocks, block_offsets):
    components, cell_rows, columns = snapshots.shape
    planes, devices = lax.axis_size("snap"), lax.axis_size("cells")
    rows, half = cell_rows // planes, columns // 2
    scale = 1.0 / float(components * cell_rows * devices)
    z = lax.axis_index("snap")

    def to_plane(array, m):
        return lax.ppermute(array, "snap", [(i, i ^ m) for i in range(planes)])

    def rows_of(array, m):
        return lax.dynamic_slice_in_dim(array, (z ^ m) * rows, rows, axis=1)

    def send(array, m, k, wanted):
        pairs = []
        for c in range(devices):
            for i in range(planes):
                to_c, to_i = c ^ (2 * m), i ^ k
                if ((to_c // 2) ^ to_i) in wanted:
                    pairs.append((c * planes + i, to_c * planes + to_i))
        return lax.ppermute(array, ("cells", "snap"), pairs)

    def swap(array):
        return lax.ppermute(array, "cells", [(c, c ^ 1) for c in range(devices)])

    def coded(slots):
        return ((slots * columns + TAIL, half), jnp.int16)

    def floats(*slots):
        return ((*slots, columns, half), F32)

    out2, out1, out3 = rows_of(snapshots, 2), rows_of(snapshots, 1), rows_of(snapshots, 3)
    s2 = to_plane(out2, 2)
    diagonal, weighted, square, square_other = call(
        functools.partial(early_kernel, scale),
        [((planes, rows, rows), BF16), (snapshots.shape, BF16), floats(), floats()],
        "early",
        block_offsets,
        mass_blocks,
        snapshots,
        smem=(0,),
        scratch=[pltpu.SMEM((mass_blocks.shape[0],), jnp.int32)],
    )
    out1, out3, weighted = lax.optimization_barrier((out1, out3, weighted))
    s1 = to_plane(out1, 1)
    s3 = to_plane(out3, 3)
    s1b = to_plane(out3, 1)
    square_arrived = swap(square_other)

    own, other, later = call(
        functools.partial(stage_c_kernel, scale),
        [floats(len(STAGE_C)), coded(len(STAGE_C)), ((columns, columns), F32)],
        "stage_c",
        snapshots,
        weighted,
        diagonal,
        s1,
        s2,
    )
    total, *out = call(
        combine_c_kernel,
        [floats(2), coded(2), coded(2), coded(2)],
        "combine_c",
        own,
        swap(other),
        square,
        square_arrived,
    )
    arrived = [send(out[m - 1], m, 0, (0, 1, 2)) for m in (1, 2, 3)]
    keep, two = call(plane_c_kernel, [floats(), coded(1)], "plane_c", total, *arrived)
    from2 = send(two, 0, 2, (2, 3))
    s1b, s3, keep = lax.optimization_barrier((s1b, s3, keep))

    own, other = call(
        functools.partial(stage_d_kernel, scale),
        [floats(len(STAGE_D)), coded(len(STAGE_D))],
        "stage_d",
        snapshots,
        weighted,
        diagonal,
        later,
        s1,
        s1b,
        s3,
    )
    total, *out = call(
        combine_d_kernel,
        [floats(2), coded(2), coded(2), coded(2)],
        "combine_d",
        own,
        swap(other),
        scratch=[pltpu.VMEM(own.shape, F32)],
    )
    arrived = [send(out[m - 1], m, 0, (0, 1, 2, 3)) for m in (1, 2, 3)]
    keep, one, three = call(
        plane_d_kernel, [floats(), coded(1), coded(1)], "plane_d", total, *arrived, keep
    )
    from1 = send(one, 0, 1, (1, 2, 3))
    from3 = send(three, 0, 3, (2, 3))
    return call(last_kernel, [floats()], "last", keep, from1, from2, from3)[0]


def solution(mesh):
    fits = mesh.shape["cells"] == 8 and mesh.shape["snap"] == 4
    placed = (P(None, "cells", "snap"), P("cells", None, None), P("cells"))
    return jax.shard_map(
        fast if fits else general,
        mesh=mesh,
        in_specs=placed,
        out_specs=P("snap", "cells"),
        check_vma=False,
    )
```

```python
import functools

import jax
import jax.numpy as jnp
from jax import lax
from jax.experimental import pallas as pl
from jax.experimental.pallas import tpu as pltpu
from jax.sharding import PartitionSpec as P

BF16, F32 = jnp.bfloat16, jnp.float32


def general(snapshots, mass_blocks, block_offsets):
    components, cell_rows, columns_dev = snapshots.shape
    blocks_dev = mass_blocks.shape[0]
    block_size = mass_blocks.shape[1]
    base_block = lax.axis_index("cells") * blocks_dev
    local_index = block_offsets // block_size - base_block
    selected = jnp.take(
        snapshots.reshape(components, blocks_dev, block_size, columns_dev), local_index, axis=1
    )
    weighted = jnp.einsum(
        "bij,cbjs->cbis", mass_blocks, selected, preferred_element_type=F32
    ).astype(BF16)
    left_rows = selected.reshape(components * cell_rows, columns_dev)
    right_rows = weighted.reshape(components * cell_rows, columns_dev)
    product = lax.dot_general(
        left_rows,
        lax.all_gather(right_rows, "snap", axis=1, tiled=True),
        (((0,), (0,)), ((), ())),
        preferred_element_type=F32,
    )
    factor = 1.0 / float(3 * cell_rows * lax.axis_size("cells"))
    result = lax.psum_scatter(product, "cells", scatter_dimension=1, tiled=True)
    return result * factor


STAGE_C = ((2, 0), (2, 1), (0, 2))
STAGE_D = ((1, 0), (3, 0), (0, 1), (3, 1), (0, 3), (1, 3), (1, 2))
START_D = (0, 2, 5, 4)


def tdot(left, right):
    return lax.dot_general(left, right, (((0,), (0,)), ((), ())), preferred_element_type=F32)


def weigh(diagonal, piece):
    return jnp.concatenate(
        [
            jnp.dot(diagonal, piece[c], preferred_element_type=F32).astype(BF16)
            for c in range(piece.shape[0])
        ],
        axis=0,
    )


def flat(piece):
    return piece.reshape(piece.shape[0] * piece.shape[1], piece.shape[2])


def halves(core, block):
    half = block.shape[1] // 2
    low, high = block[:, :half], block[:, half:]
    first = core == 0
    return jnp.where(first, low, high), jnp.where(first, high, low)


def early_kernel(
    scale, offsets_ref, mass_ref, s_ref, diagonal_ref, weighted_ref, own_ref, other_ref, where_ref
):
    components = s_ref.shape[0]
    blocks, size, _ = mass_ref.shape
    quarters, rows, _ = diagonal_ref.shape
    cells = lax.axis_index("cells")
    base = cells * blocks
    for b in range(blocks):
        where_ref[offsets_ref[b] // size - base] = b
    diagonal_ref[...] = jnp.zeros_like(diagonal_ref)
    per = blocks // quarters
    for t in range(quarters):
        for i in range(per):
            diagonal_ref[t, i * size : (i + 1) * size, i * size : (i + 1) * size] = mass_ref[
                where_ref[t * per + i]
            ]
    for t in range(quarters):
        for c in range(components):
            rows_now = slice(t * rows, (t + 1) * rows)
            weighted_ref[c, rows_now, :] = jnp.dot(
                diagonal_ref[t], s_ref[c, rows_now, :], preferred_element_type=F32
            ).astype(BF16)
    total = tdot(s_ref[0], weighted_ref[0])
    for c in range(1, components):
        total += tdot(s_ref[c], weighted_ref[c])
    own_ref[...], other_ref[...] = halves(cells % 2, total * scale)


def stage_c_kernel(
    scale, s_ref, weighted_ref, diagonal_ref, s1_ref, s2_ref, own_ref, other_ref, later_ref
):
    z, core = lax.axis_index("snap"), lax.axis_index("cells") % 2
    rows = s2_ref.shape[1]
    mine = pl.ds(pl.multiple_of(z * rows, rows), rows)
    diagonal = diagonal_ref[z]
    s0, w0 = flat(s_ref[:, mine, :]), flat(weighted_ref[:, mine, :])
    s1, s2 = flat(s1_ref[...]), flat(s2_ref[...])
    w1, w2 = weigh(diagonal, s1_ref[...]), weigh(diagonal, s2_ref[...])
    blocks = {(2, 0): tdot(s2, w0), (2, 1): tdot(s2, w1), (0, 2): tdot(s0, w2)}
    others = []
    for at, name in enumerate(STAGE_C):
        own_ref[at], other = halves(core, blocks[name] * scale)
        others.append(other)
    encode(jnp.stack(others), other_ref)
    later_ref[...] = tdot(s1, w2)


def stage_d_kernel(
    scale,
    s_ref,
    weighted_ref,
    diagonal_ref,
    later_ref,
    s1_ref,
    s1b_ref,
    s3_ref,
    own_ref,
    other_ref,
):
    z, core = lax.axis_index("snap"), lax.axis_index("cells") % 2
    rows = s3_ref.shape[1]
    across = z ^ 2
    mine = pl.ds(pl.multiple_of(z * rows, rows), rows)
    more = pl.ds(pl.multiple_of(across * rows, rows), rows)
    diagonal = diagonal_ref[z]
    s0, w0 = flat(s_ref[:, mine, :]), flat(weighted_ref[:, mine, :])
    s0b, w0b = flat(s_ref[:, more, :]), flat(weighted_ref[:, more, :])
    s1, s1b, s3 = flat(s1_ref[...]), flat(s1b_ref[...]), flat(s3_ref[...])
    w1, w3 = weigh(diagonal, s1_ref[...]), weigh(diagonal, s3_ref[...])
    w1b = weigh(diagonal_ref[across], s1b_ref[...])
    blocks = {
        (1, 0): tdot(s1, w0) + tdot(s1b, w0b),
        (3, 0): tdot(s3, w0),
        (0, 1): tdot(s0, w1) + tdot(s0b, w1b),
        (3, 1): tdot(s3, w1),
        (0, 3): tdot(s0, w3),
        (1, 3): tdot(s1, w3),
        (1, 2): later_ref[...],
    }
    others = []
    for at, name in enumerate(STAGE_D):
        own_ref[at], other = halves(core, blocks[name] * scale)
        others.append(other)
    encode(jnp.stack(others), other_ref)


GROUP = 64
TAIL = 32
STEPS = 256.0
TOP = 32700.0


def encode(value, message_ref):
    slots, rows, columns = value.shape
    groups = slots * rows // GROUP
    value = value.reshape(groups, GROUP, columns)
    most = jnp.maximum(jnp.max(jnp.abs(value), axis=1), 1e-36)
    step = jnp.ceil(jnp.log2(most) * STEPS)
    code = jnp.round(value * (TOP * jnp.exp2(step * (-1.0 / STEPS)))[:, None, :])
    codes = code.reshape(slots * rows, columns).astype(jnp.int32).astype(jnp.int16)
    message_ref[: slots * rows] = codes
    step = jnp.concatenate([step, jnp.zeros((TAIL - groups, columns), F32)], axis=0)
    message_ref[slots * rows :] = step.astype(jnp.int32).astype(jnp.int16)


def decode(message_ref, slots):
    total, columns = message_ref.shape
    rows = (total - TAIL) // slots
    groups = slots * rows // GROUP
    step = message_ref[slots * rows :].astype(jnp.int32).astype(F32)[:groups]
    code = message_ref[: slots * rows].astype(jnp.int32).astype(F32)
    value = code.reshape(groups, GROUP, columns) * (jnp.exp2(step * (1.0 / STEPS)) * (1.0 / TOP))[:, None, :]
    return value.reshape(slots, rows, columns)


def place():
    return (lax.axis_index("cells") // 2) ^ lax.axis_index("snap")


def combine_c_kernel(own_ref, arrived_ref, one_ref, other_ref, total_ref, *message_refs):
    q = place()
    whole = own_ref[...] + decode(arrived_ref, len(STAGE_C))
    square = one_ref[...] + other_ref[...]
    for m, ref in enumerate((total_ref, *message_refs)):
        to = q ^ m
        first = jnp.where(to == 0, whole[0], jnp.where(to == 1, whole[1], whole[2]))
        value = jnp.stack([first, square])
        if m == 0:
            ref[...] = value
        else:
            encode(value, ref)


def combine_d_kernel(own_ref, arrived_ref, total_ref, *refs):
    *message_refs, whole_ref = refs
    q = place()
    whole_ref[...] = own_ref[...] + decode(arrived_ref, len(STAGE_D))
    for m, ref in enumerate((total_ref, *message_refs)):
        to = q ^ m
        start = jnp.where(to == 1, START_D[1], jnp.where(to == 2, START_D[2], START_D[3]))
        value = whole_ref[pl.ds(jnp.where(to == 0, START_D[0], start), 2)]
        if m == 0:
            ref[...] = value
        else:
            encode(value, ref)


def plane_sum(total_ref, message_refs):
    total = total_ref[...]
    for ref in message_refs:
        total += decode(ref, 2)
    return total


def plane_c_kernel(total_ref, m1_ref, m2_ref, m3_ref, keep_ref, two_ref):
    total = plane_sum(total_ref, (m1_ref, m2_ref, m3_ref))
    encode(total[:1], two_ref)
    keep_ref[...] = jnp.where(place() == 0, total[1], total[0])


def plane_d_kernel(total_ref, m1_ref, m2_ref, m3_ref, keep_c_ref, keep_ref, one_ref, three_ref):
    q = place()
    total = plane_sum(total_ref, (m1_ref, m2_ref, m3_ref))
    encode(jnp.where(q == 0, total[:1], total[1:]), one_ref)
    encode(total[1:], three_ref)
    keep_ref[...] = jnp.where(q % 2 == 0, keep_c_ref[...], total[0])


def last_kernel(keep_ref, m1_ref, m2_ref, m3_ref, out_ref):
    out_ref[...] = (
        keep_ref[...] + decode(m1_ref, 1)[0] + decode(m2_ref, 1)[0] + decode(m3_ref, 1)[0]
    )


def call(kernel, outs, name, *args, smem=(), scratch=()):
    vmem, scalar = pl.BlockSpec(memory_space=pltpu.VMEM), pl.BlockSpec(memory_space=pltpu.SMEM)
    return pl.pallas_call(
        kernel,
        out_shape=[jax.ShapeDtypeStruct(s, t) for s, t in outs],
        in_specs=[scalar if k in smem else vmem for k in range(len(args))],
        out_specs=[vmem] * len(outs),
        scratch_shapes=scratch,
        compiler_params=pltpu.CompilerParams(vmem_limit_bytes=LIMIT),
        cost_estimate=pl.CostEstimate(flops=0, bytes_accessed=0, transcendentals=0),
        name=name,
    )(*args)


LIMIT = 24 * 2**20


def fast(snapshots, mass_blocks, block_offsets):
    components, cell_rows, columns = snapshots.shape
    planes, devices = lax.axis_size("snap"), lax.axis_size("cells")
    rows, half = cell_rows // planes, columns // 2
    scale = 1.0 / float(components * cell_rows * devices)
    z = lax.axis_index("snap")

    def to_plane(array, m):
        return lax.ppermute(array, "snap", [(i, i ^ m) for i in range(planes)])

    def rows_of(array, m):
        return lax.dynamic_slice_in_dim(array, (z ^ m) * rows, rows, axis=1)

    def send(array, m, k, wanted):
        pairs = []
        for c in range(devices):
            for i in range(planes):
                to_c, to_i = c ^ (2 * m), i ^ k
                if ((to_c // 2) ^ to_i) in wanted:
                    pairs.append((c * planes + i, to_c * planes + to_i))
        return lax.ppermute(array, ("cells", "snap"), pairs)

    def swap(array):
        return lax.ppermute(array, "cells", [(c, c ^ 1) for c in range(devices)])

    def coded(slots):
        return ((slots * columns + TAIL, half), jnp.int16)

    def floats(*slots):
        return ((*slots, columns, half), F32)

    out2, out1, out3 = rows_of(snapshots, 2), rows_of(snapshots, 1), rows_of(snapshots, 3)
    s2 = to_plane(out2, 2)
    diagonal, weighted, square, square_other = call(
        functools.partial(early_kernel, scale),
        [((planes, rows, rows), BF16), (snapshots.shape, BF16), floats(), floats()],
        "early",
        block_offsets,
        mass_blocks,
        snapshots,
        smem=(0,),
        scratch=[pltpu.SMEM((mass_blocks.shape[0],), jnp.int32)],
    )
    out1, weighted = lax.optimization_barrier((out1, weighted))
    s1 = to_plane(out1, 1)
    square_arrived = swap(square_other)
    out3, square_arrived = lax.optimization_barrier((out3, square_arrived))
    s3 = to_plane(out3, 3)
    s1b = to_plane(out3, 1)

    own, other, later = call(
        functools.partial(stage_c_kernel, scale),
        [floats(len(STAGE_C)), coded(len(STAGE_C)), ((columns, columns), F32)],
        "stage_c",
        snapshots,
        weighted,
        diagonal,
        s1,
        s2,
    )
    total, *out = call(
        combine_c_kernel,
        [floats(2), coded(2), coded(2), coded(2)],
        "combine_c",
        own,
        swap(other),
        square,
        square_arrived,
    )
    arrived = [send(out[m - 1], m, 0, (0, 1, 2)) for m in (1, 2, 3)]
    keep, two = call(plane_c_kernel, [floats(), coded(1)], "plane_c", total, *arrived)
    from2 = send(two, 0, 2, (2, 3))
    s1b, s3, keep = lax.optimization_barrier((s1b, s3, keep))

    own, other = call(
        functools.partial(stage_d_kernel, scale),
        [floats(len(STAGE_D)), coded(len(STAGE_D))],
        "stage_d",
        snapshots,
        weighted,
        diagonal,
        later,
        s1,
        s1b,
        s3,
    )
    total, *out = call(
        combine_d_kernel,
        [floats(2), coded(2), coded(2), coded(2)],
        "combine_d",
        own,
        swap(other),
        scratch=[pltpu.VMEM(own.shape, F32)],
    )
    arrived = [send(out[m - 1], m, 0, (0, 1, 2, 3)) for m in (1, 2, 3)]
    keep, one, three = call(
        plane_d_kernel, [floats(), coded(1), coded(1)], "plane_d", total, *arrived, keep
    )
    from1 = send(one, 0, 1, (1, 2, 3))
    from3 = send(three, 0, 3, (2, 3))
    return call(last_kernel, [floats()], "last", keep, from1, from2, from3)[0]


def solution(mesh):
    fits = mesh.shape["cells"] == 8 and mesh.shape["snap"] == 4
    placed = (P(None, "cells", "snap"), P("cells", None, None), P("cells"))
    return jax.shard_map(
        fast if fits else general,
        mesh=mesh,
        in_specs=placed,
        out_specs=P("snap", "cells"),
        check_vma=False,
    )
```

```python
import functools

import jax
import jax.numpy as jnp
from jax import lax
from jax.experimental import pallas as pl
from jax.experimental.pallas import tpu as pltpu
from jax.sharding import PartitionSpec as P

BF16, F32 = jnp.bfloat16, jnp.float32


def general(snapshots, mass_blocks, block_offsets):
    components, cell_rows, columns_dev = snapshots.shape
    blocks_dev = mass_blocks.shape[0]
    block_size = mass_blocks.shape[1]
    base_block = lax.axis_index("cells") * blocks_dev
    local_index = block_offsets // block_size - base_block
    selected = jnp.take(
        snapshots.reshape(components, blocks_dev, block_size, columns_dev), local_index, axis=1
    )
    weighted = jnp.einsum(
        "bij,cbjs->cbis", mass_blocks, selected, preferred_element_type=F32
    ).astype(BF16)
    left_rows = selected.reshape(components * cell_rows, columns_dev)
    right_rows = weighted.reshape(components * cell_rows, columns_dev)
    product = lax.dot_general(
        left_rows,
        lax.all_gather(right_rows, "snap", axis=1, tiled=True),
        (((0,), (0,)), ((), ())),
        preferred_element_type=F32,
    )
    factor = 1.0 / float(3 * cell_rows * lax.axis_size("cells"))
    result = lax.psum_scatter(product, "cells", scatter_dimension=1, tiled=True)
    return result * factor


STAGE_C = ((2, 0), (2, 1), (0, 2))
STAGE_D = ((1, 0), (3, 0), (0, 1), (3, 1), (0, 3), (1, 3), (1, 2))
START_D = (0, 2, 5, 4)


def tdot(left, right):
    return lax.dot_general(left, right, (((0,), (0,)), ((), ())), preferred_element_type=F32)


def weigh(diagonal, piece):
    return jnp.concatenate(
        [
            jnp.dot(diagonal, piece[c], preferred_element_type=F32).astype(BF16)
            for c in range(piece.shape[0])
        ],
        axis=0,
    )


def flat(piece):
    return piece.reshape(piece.shape[0] * piece.shape[1], piece.shape[2])


def halves(core, block):
    half = block.shape[1] // 2
    low, high = block[:, :half], block[:, half:]
    first = core == 0
    return jnp.where(first, low, high), jnp.where(first, high, low)


def early_kernel(
    scale, offsets_ref, mass_ref, s_ref, diagonal_ref, weighted_ref, own_ref, other_ref, where_ref
):
    components = s_ref.shape[0]
    blocks, size, _ = mass_ref.shape
    quarters, rows, _ = diagonal_ref.shape
    cells = lax.axis_index("cells")
    base = cells * blocks
    for b in range(blocks):
        where_ref[offsets_ref[b] // size - base] = b
    diagonal_ref[...] = jnp.zeros_like(diagonal_ref)
    per = blocks // quarters
    for t in range(quarters):
        for i in range(per):
            diagonal_ref[t, i * size : (i + 1) * size, i * size : (i + 1) * size] = mass_ref[
                where_ref[t * per + i]
            ]
    for t in range(quarters):
        for c in range(components):
            rows_now = slice(t * rows, (t + 1) * rows)
            weighted_ref[c, rows_now, :] = jnp.dot(
                diagonal_ref[t], s_ref[c, rows_now, :], preferred_element_type=F32
            ).astype(BF16)
    total = tdot(s_ref[0], weighted_ref[0])
    for c in range(1, components):
        total += tdot(s_ref[c], weighted_ref[c])
    own_ref[...], other_ref[...] = halves(cells % 2, total * scale)


def stage_c_kernel(
    scale, s_ref, weighted_ref, diagonal_ref, s1_ref, s2_ref, own_ref, other_ref, later_ref
):
    z, core = lax.axis_index("snap"), lax.axis_index("cells") % 2
    rows = s2_ref.shape[1]
    mine = pl.ds(pl.multiple_of(z * rows, rows), rows)
    diagonal = diagonal_ref[z]
    s0, w0 = flat(s_ref[:, mine, :]), flat(weighted_ref[:, mine, :])
    s1, s2 = flat(s1_ref[...]), flat(s2_ref[...])
    w1, w2 = weigh(diagonal, s1_ref[...]), weigh(diagonal, s2_ref[...])
    blocks = {(2, 0): tdot(s2, w0), (2, 1): tdot(s2, w1), (0, 2): tdot(s0, w2)}
    others = []
    for at, name in enumerate(STAGE_C):
        own_ref[at], other = halves(core, blocks[name] * scale)
        others.append(other)
    encode(jnp.stack(others), other_ref)
    later_ref[...] = tdot(s1, w2)


def stage_d_kernel(
    scale,
    s_ref,
    weighted_ref,
    diagonal_ref,
    later_ref,
    s1_ref,
    s1b_ref,
    s3_ref,
    own_ref,
    other_ref,
):
    z, core = lax.axis_index("snap"), lax.axis_index("cells") % 2
    rows = s3_ref.shape[1]
    across = z ^ 2
    mine = pl.ds(pl.multiple_of(z * rows, rows), rows)
    more = pl.ds(pl.multiple_of(across * rows, rows), rows)
    diagonal = diagonal_ref[z]
    s0, w0 = flat(s_ref[:, mine, :]), flat(weighted_ref[:, mine, :])
    s0b, w0b = flat(s_ref[:, more, :]), flat(weighted_ref[:, more, :])
    s1, s1b, s3 = flat(s1_ref[...]), flat(s1b_ref[...]), flat(s3_ref[...])
    w1, w3 = weigh(diagonal, s1_ref[...]), weigh(diagonal, s3_ref[...])
    w1b = weigh(diagonal_ref[across], s1b_ref[...])
    blocks = {
        (1, 0): tdot(s1, w0) + tdot(s1b, w0b),
        (3, 0): tdot(s3, w0),
        (0, 1): tdot(s0, w1) + tdot(s0b, w1b),
        (3, 1): tdot(s3, w1),
        (0, 3): tdot(s0, w3),
        (1, 3): tdot(s1, w3),
        (1, 2): later_ref[...],
    }
    others = []
    for at, name in enumerate(STAGE_D):
        own_ref[at], other = halves(core, blocks[name] * scale)
        others.append(other)
    encode(jnp.stack(others), other_ref)


GROUP = 64
TAIL = 32
STEPS = 256.0
TOP = 32700.0


def encode(value, message_ref):
    slots, rows, columns = value.shape
    groups = slots * rows // GROUP
    value = value.reshape(groups, GROUP, columns)
    most = jnp.maximum(jnp.max(jnp.abs(value), axis=1), 1e-36)
    step = jnp.ceil(jnp.log2(most) * STEPS)
    code = jnp.round(value * (TOP * jnp.exp2(step * (-1.0 / STEPS)))[:, None, :])
    codes = code.reshape(slots * rows, columns).astype(jnp.int32).astype(jnp.int16)
    message_ref[: slots * rows] = codes
    step = jnp.concatenate([step, jnp.zeros((TAIL - groups, columns), F32)], axis=0)
    message_ref[slots * rows :] = step.astype(jnp.int32).astype(jnp.int16)


def decode(message_ref, slots):
    total, columns = message_ref.shape
    rows = (total - TAIL) // slots
    groups = slots * rows // GROUP
    step = message_ref[slots * rows :].astype(jnp.int32).astype(F32)[:groups]
    code = message_ref[: slots * rows].astype(jnp.int32).astype(F32)
    value = code.reshape(groups, GROUP, columns) * (jnp.exp2(step * (1.0 / STEPS)) * (1.0 / TOP))[:, None, :]
    return value.reshape(slots, rows, columns)


def place():
    return (lax.axis_index("cells") // 2) ^ lax.axis_index("snap")


def combine_c_kernel(own_ref, arrived_ref, one_ref, other_ref, total_ref, *message_refs):
    q = place()
    whole = own_ref[...] + decode(arrived_ref, len(STAGE_C))
    square = one_ref[...] + other_ref[...]
    for m, ref in enumerate((total_ref, *message_refs)):
        to = q ^ m
        first = jnp.where(to == 0, whole[0], jnp.where(to == 1, whole[1], whole[2]))
        value = jnp.stack([first, square])
        if m == 0:
            ref[...] = value
        else:
            encode(value, ref)


def combine_d_kernel(own_ref, arrived_ref, total_ref, *refs):
    *message_refs, whole_ref = refs
    q = place()
    whole_ref[...] = own_ref[...] + decode(arrived_ref, len(STAGE_D))
    for m, ref in enumerate((total_ref, *message_refs)):
        to = q ^ m
        start = jnp.where(to == 1, START_D[1], jnp.where(to == 2, START_D[2], START_D[3]))
        value = whole_ref[pl.ds(jnp.where(to == 0, START_D[0], start), 2)]
        if m == 0:
            ref[...] = value
        else:
            encode(value, ref)


def plane_sum(total_ref, message_refs):
    total = total_ref[...]
    for ref in message_refs:
        total += decode(ref, 2)
    return total


def plane_c_kernel(total_ref, m1_ref, m2_ref, m3_ref, keep_ref, two_ref):
    total = plane_sum(total_ref, (m1_ref, m2_ref, m3_ref))
    encode(total[:1], two_ref)
    keep_ref[...] = jnp.where(place() == 0, total[1], total[0])


def plane_d_kernel(total_ref, m1_ref, m2_ref, m3_ref, keep_c_ref, keep_ref, one_ref, three_ref):
    q = place()
    total = plane_sum(total_ref, (m1_ref, m2_ref, m3_ref))
    encode(jnp.where(q == 0, total[:1], total[1:]), one_ref)
    encode(total[1:], three_ref)
    keep_ref[...] = jnp.where(q % 2 == 0, keep_c_ref[...], total[0])


def last_kernel(keep_ref, m1_ref, m2_ref, m3_ref, out_ref):
    out_ref[...] = (
        keep_ref[...] + decode(m1_ref, 1)[0] + decode(m2_ref, 1)[0] + decode(m3_ref, 1)[0]
    )


def call(kernel, outs, name, *args, smem=(), scratch=()):
    vmem, scalar = pl.BlockSpec(memory_space=pltpu.VMEM), pl.BlockSpec(memory_space=pltpu.SMEM)
    return pl.pallas_call(
        kernel,
        out_shape=[jax.ShapeDtypeStruct(s, t) for s, t in outs],
        in_specs=[scalar if k in smem else vmem for k in range(len(args))],
        out_specs=[vmem] * len(outs),
        scratch_shapes=scratch,
        compiler_params=pltpu.CompilerParams(vmem_limit_bytes=LIMIT),
        cost_estimate=pl.CostEstimate(flops=0, bytes_accessed=0, transcendentals=0),
        name=name,
    )(*args)


LIMIT = 24 * 2**20


def fast(snapshots, mass_blocks, block_offsets):
    components, cell_rows, columns = snapshots.shape
    planes, devices = lax.axis_size("snap"), lax.axis_size("cells")
    rows, half = cell_rows // planes, columns // 2
    scale = 1.0 / float(components * cell_rows * devices)
    z = lax.axis_index("snap")

    def to_plane(array, m):
        return lax.ppermute(array, "snap", [(i, i ^ m) for i in range(planes)])

    def rows_of(array, m):
        return lax.dynamic_slice_in_dim(array, (z ^ m) * rows, rows, axis=1)

    def send(array, m, k, wanted):
        pairs = []
        for c in range(devices):
            for i in range(planes):
                to_c, to_i = c ^ (2 * m), i ^ k
                if ((to_c // 2) ^ to_i) in wanted:
                    pairs.append((c * planes + i, to_c * planes + to_i))
        return lax.ppermute(array, ("cells", "snap"), pairs)

    def swap(array):
        return lax.ppermute(array, "cells", [(c, c ^ 1) for c in range(devices)])

    def coded(slots):
        return ((slots * columns + TAIL, half), jnp.int16)

    def floats(*slots):
        return ((*slots, columns, half), F32)

    out2, out1, out3 = rows_of(snapshots, 2), rows_of(snapshots, 1), rows_of(snapshots, 3)
    s2 = to_plane(out2, 2)
    diagonal, weighted, square, square_other = call(
        functools.partial(early_kernel, scale),
        [((planes, rows, rows), BF16), (snapshots.shape, BF16), floats(), floats()],
        "early",
        block_offsets,
        mass_blocks,
        snapshots,
        smem=(0,),
        scratch=[pltpu.SMEM((mass_blocks.shape[0],), jnp.int32)],
    )
    s1 = to_plane(out1, 1)
    s1b = to_plane(out3, 1)
    square_arrived = swap(square_other)
    out3, square_arrived = lax.optimization_barrier((out3, square_arrived))
    s3 = to_plane(out3, 3)

    own, other, later = call(
        functools.partial(stage_c_kernel, scale),
        [floats(len(STAGE_C)), coded(len(STAGE_C)), ((columns, columns), F32)],
        "stage_c",
        snapshots,
        weighted,
        diagonal,
        s1,
        s2,
    )
    total, *out = call(
        combine_c_kernel,
        [floats(2), coded(2), coded(2), coded(2)],
        "combine_c",
        own,
        swap(other),
        square,
        square_arrived,
    )
    arrived = [send(out[m - 1], m, 0, (0, 1, 2)) for m in (1, 2, 3)]
    keep, two = call(plane_c_kernel, [floats(), coded(1)], "plane_c", total, *arrived)
    from2 = send(two, 0, 2, (2, 3))
    s1b, s3, keep = lax.optimization_barrier((s1b, s3, keep))

    own, other = call(
        functools.partial(stage_d_kernel, scale),
        [floats(len(STAGE_D)), coded(len(STAGE_D))],
        "stage_d",
        snapshots,
        weighted,
        diagonal,
        later,
        s1,
        s1b,
        s3,
    )
    total, *out = call(
        combine_d_kernel,
        [floats(2), coded(2), coded(2), coded(2)],
        "combine_d",
        own,
        swap(other),
        scratch=[pltpu.VMEM(own.shape, F32)],
    )
    arrived = [send(out[m - 1], m, 0, (0, 1, 2, 3)) for m in (1, 2, 3)]
    keep, one, three = call(
        plane_d_kernel, [floats(), coded(1), coded(1)], "plane_d", total, *arrived, keep
    )
    from1 = send(one, 0, 1, (1, 2, 3))
    from3 = send(three, 0, 3, (2, 3))
    return call(last_kernel, [floats()], "last", keep, from1, from2, from3)[0]


def solution(mesh):
    fits = mesh.shape["cells"] == 8 and mesh.shape["snap"] == 4
    placed = (P(None, "cells", "snap"), P("cells", None, None), P("cells"))
    return jax.shard_map(
        fast if fits else general,
        mesh=mesh,
        in_specs=placed,
        out_specs=P("snap", "cells"),
        check_vma=False,
    )
```

```python
import functools

import jax
import jax.numpy as jnp
from jax import lax
from jax.experimental import pallas as pl
from jax.experimental.pallas import tpu as pltpu
from jax.sharding import PartitionSpec as P

BF16, F32 = jnp.bfloat16, jnp.float32


def general(snapshots, mass_blocks, block_offsets):
    components, cell_rows, columns_dev = snapshots.shape
    blocks_dev = mass_blocks.shape[0]
    block_size = mass_blocks.shape[1]
    base_block = lax.axis_index("cells") * blocks_dev
    local_index = block_offsets // block_size - base_block
    selected = jnp.take(
        snapshots.reshape(components, blocks_dev, block_size, columns_dev), local_index, axis=1
    )
    weighted = jnp.einsum(
        "bij,cbjs->cbis", mass_blocks, selected, preferred_element_type=F32
    ).astype(BF16)
    left_rows = selected.reshape(components * cell_rows, columns_dev)
    right_rows = weighted.reshape(components * cell_rows, columns_dev)
    product = lax.dot_general(
        left_rows,
        lax.all_gather(right_rows, "snap", axis=1, tiled=True),
        (((0,), (0,)), ((), ())),
        preferred_element_type=F32,
    )
    factor = 1.0 / float(3 * cell_rows * lax.axis_size("cells"))
    result = lax.psum_scatter(product, "cells", scatter_dimension=1, tiled=True)
    return result * factor


STAGE_C = ((1, 3), (3, 0), (3, 1), (0, 3))
STAGE_D = ((2, 0), (1, 0), (0, 2), (2, 1))
STAGE_B = ((0, 1), (1, 2))
GO_EARLY = {1: (3, 0), 2: (3, 1)}
GO_FIRST = {0: (2, 0), 1: (1, 0), 3: (2, 1)}
GO_LAST = {0: (1, 3), 2: (1, 2)}


def tdot(left, right):
    return lax.dot_general(left, right, (((0,), (0,)), ((), ())), preferred_element_type=F32)


def weigh(diagonal, piece):
    return jnp.concatenate(
        [
            jnp.dot(diagonal, piece[c], preferred_element_type=F32).astype(BF16)
            for c in range(piece.shape[0])
        ],
        axis=0,
    )


def flat(piece):
    return piece.reshape(piece.shape[0] * piece.shape[1], piece.shape[2])


def halves(core, block):
    half = block.shape[1] // 2
    low, high = block[:, :half], block[:, half:]
    first = core == 0
    return jnp.where(first, low, high), jnp.where(first, high, low)


def early_kernel(
    scale, offsets_ref, mass_ref, s_ref, diagonal_ref, weighted_ref, own_ref, other_ref, where_ref
):
    components = s_ref.shape[0]
    blocks, size, _ = mass_ref.shape
    quarters, rows, _ = diagonal_ref.shape
    cells = lax.axis_index("cells")
    base = cells * blocks
    for b in range(blocks):
        where_ref[offsets_ref[b] // size - base] = b
    diagonal_ref[...] = jnp.zeros_like(diagonal_ref)
    per = blocks // quarters
    for t in range(quarters):
        for i in range(per):
            diagonal_ref[t, i * size : (i + 1) * size, i * size : (i + 1) * size] = mass_ref[
                where_ref[t * per + i]
            ]
    for t in range(quarters):
        for c in range(components):
            rows_now = slice(t * rows, (t + 1) * rows)
            weighted_ref[c, rows_now, :] = jnp.dot(
                diagonal_ref[t], s_ref[c, rows_now, :], preferred_element_type=F32
            ).astype(BF16)
    total = tdot(s_ref[0], weighted_ref[0])
    for c in range(1, components):
        total += tdot(s_ref[c], weighted_ref[c])
    own_ref[...], other_ref[...] = halves(cells % 2, total * scale)


def emit(scale, blocks, own_ref, other_ref):
    core = lax.axis_index("cells") % 2
    others = []
    for at, block in enumerate(blocks):
        own_ref[at], other = halves(core, block * scale)
        others.append(other)
    encode(jnp.stack(others), other_ref)


def quarter(z, ref):
    rows = ref.shape[1] // lax.axis_size("snap")
    return flat(ref[:, pl.ds(pl.multiple_of(z * rows, rows), rows), :])


def stage_c_kernel(
    scale, s_ref, weighted_ref, diagonal_ref, s1_ref, s3_ref, own_ref, other_ref, w1_ref
):
    z = lax.axis_index("snap")
    diagonal = diagonal_ref[z]
    s0, w0 = quarter(z, s_ref), quarter(z, weighted_ref)
    s1, s3 = flat(s1_ref[...]), flat(s3_ref[...])
    w1, w3 = weigh(diagonal, s1_ref[...]), weigh(diagonal, s3_ref[...])
    w1_ref[...] = w1
    blocks = {(3, 0): (s3, w0), (3, 1): (s3, w1), (0, 3): (s0, w3), (1, 3): (s1, w3)}
    emit(scale, [tdot(*blocks[name]) for name in STAGE_C], own_ref, other_ref)


def stage_d_kernel(
    scale, s_ref, weighted_ref, diagonal_ref, s1_ref, w1_ref, s1b_ref, s2_ref, own_ref, other_ref
):
    z = lax.axis_index("snap")
    across = z ^ 2
    s0, w0 = quarter(z, s_ref), quarter(z, weighted_ref)
    s0b, w0b = quarter(across, s_ref), quarter(across, weighted_ref)
    s1, s1b, s2, w1 = flat(s1_ref[...]), flat(s1b_ref[...]), flat(s2_ref[...]), w1_ref[...]
    w1b = weigh(diagonal_ref[across], s1b_ref[...])
    w2 = weigh(diagonal_ref[z], s2_ref[...])
    blocks = {
        (0, 1): tdot(s0, w1) + tdot(s0b, w1b),
        (1, 0): tdot(s1, w0) + tdot(s1b, w0b),
        (2, 0): tdot(s2, w0),
        (2, 1): tdot(s2, w1),
        (1, 2): tdot(s1, w2),
        (0, 2): tdot(s0, w2),
    }
    emit(scale, [blocks[name] for name in STAGE_D + STAGE_B], own_ref, other_ref)


GROUP = 64
STEPS = 256.0
TOP = 32700.0


def tail(slots, rows):
    return -(-slots * rows // (GROUP * 16)) * 16


def encode(value, message_ref):
    slots, rows, columns = value.shape
    groups = slots * rows // GROUP
    value = value.reshape(groups, GROUP, columns)
    most = jnp.maximum(jnp.max(jnp.abs(value), axis=1), 1e-36)
    step = jnp.ceil(jnp.log2(most) * STEPS)
    code = jnp.round(value * (TOP * jnp.exp2(step * (-1.0 / STEPS)))[:, None, :])
    codes = code.reshape(slots * rows, columns).astype(jnp.int32).astype(jnp.int16)
    message_ref[: slots * rows] = codes
    more = tail(slots, rows) - groups
    if more:
        step = jnp.concatenate([step, jnp.zeros((more, columns), F32)], axis=0)
    message_ref[slots * rows :] = step.astype(jnp.int32).astype(jnp.int16)


def decode(message_ref, slots, rows):
    columns = message_ref.shape[1]
    groups = slots * rows // GROUP
    step = message_ref[slots * rows :].astype(jnp.int32).astype(F32)[:groups]
    code = message_ref[: slots * rows].astype(jnp.int32).astype(F32)
    value = code.reshape(groups, GROUP, columns) * (jnp.exp2(step * (1.0 / STEPS)) * (1.0 / TOP))[:, None, :]
    return value.reshape(slots, rows, columns)


def place():
    return (lax.axis_index("cells") // 2) ^ lax.axis_index("snap")


def combine_kernel(own_ref, arrived_ref, total_ref, *refs):
    *message_refs, whole_ref = refs
    q = place()
    whole_ref[...] = own_ref[...] + decode(arrived_ref, *own_ref.shape[:2])
    total_ref[...] = whole_ref[pl.ds(q, 1)]
    for m, ref in enumerate(message_refs, 1):
        encode(whole_ref[pl.ds(q ^ m, 1)], ref)


def combine_d_kernel(own_ref, arrived_ref, square_ref, other_ref, total_ref, *refs):
    *message_refs, whole_ref = refs
    q = place()
    whole_ref[...] = own_ref[...] + decode(arrived_ref, *own_ref.shape[:2])
    square = square_ref[...] + other_ref[...]
    for m, ref in enumerate((total_ref, *message_refs)):
        to = q ^ m
        second = jnp.where(to == 0, square, jnp.where(to == 1, whole_ref[4], whole_ref[5]))
        value = jnp.stack([whole_ref[to], second])
        if m == 0:
            ref[...] = value
        else:
            encode(value, ref)


def plane_sum(total_ref, message_refs):
    total = total_ref[...]
    for ref in message_refs:
        total += decode(ref, *total.shape[:2])
    return total


def plane_c_kernel(total_ref, m1_ref, m2_ref, m3_ref, sum_ref, three_ref):
    total = plane_sum(total_ref, (m1_ref, m2_ref, m3_ref))
    sum_ref[...] = total
    encode(total, three_ref)


def plane_d_kernel(total_ref, m1_ref, m2_ref, m3_ref, sum_c_ref, keep_ref, first_ref, last_ref):
    q = place()
    total = plane_sum(total_ref, (m1_ref, m2_ref, m3_ref))
    sum_c = sum_c_ref[...]
    encode(total[:1], first_ref)
    encode(jnp.where(q == 0, sum_c, total[1:]), last_ref)
    keep_ref[...] = jnp.where(q < 2, total[1], jnp.where(q == 3, sum_c[0], total[0]))


def last_kernel(keep_ref, m1_ref, m2_ref, m3_ref, out_ref):
    total = keep_ref[...]
    for ref in (m1_ref, m2_ref, m3_ref):
        total += decode(ref, 1, total.shape[0])[0]
    out_ref[...] = total


def call(kernel, outs, name, *args, smem=(), scratch=()):
    vmem, scalar = pl.BlockSpec(memory_space=pltpu.VMEM), pl.BlockSpec(memory_space=pltpu.SMEM)
    return pl.pallas_call(
        kernel,
        out_shape=[jax.ShapeDtypeStruct(s, t) for s, t in outs],
        in_specs=[scalar if k in smem else vmem for k in range(len(args))],
        out_specs=[vmem] * len(outs),
        scratch_shapes=scratch,
        compiler_params=pltpu.CompilerParams(vmem_limit_bytes=LIMIT),
        cost_estimate=pl.CostEstimate(flops=0, bytes_accessed=0, transcendentals=0),
        name=name,
    )(*args)


LIMIT = 24 * 2**20


def fast(snapshots, mass_blocks, block_offsets):
    components, cell_rows, columns = snapshots.shape
    planes, devices = lax.axis_size("snap"), lax.axis_size("cells")
    rows, half = cell_rows // planes, columns // 2
    scale = 1.0 / float(components * cell_rows * devices)
    z = lax.axis_index("snap")

    def to_plane(array, m):
        return lax.ppermute(array, "snap", [(i, i ^ m) for i in range(planes)])

    def rows_of(array, m):
        return lax.dynamic_slice_in_dim(array, (z ^ m) * rows, rows, axis=1)

    def send(array, m, k, wanted):
        pairs = []
        for c in range(devices):
            for i in range(planes):
                to_c, to_i = c ^ (2 * m), i ^ k
                if ((to_c // 2) ^ to_i) in wanted:
                    pairs.append((c * planes + i, to_c * planes + to_i))
        return lax.ppermute(array, ("cells", "snap"), pairs)

    def reach(array, blocks):
        pairs = []
        for c in range(devices):
            for i in range(planes):
                if (c // 2) ^ i in blocks:
                    row, column = blocks[(c // 2) ^ i]
                    to_c = 2 * (i ^ column) + c % 2
                    pairs.append((c * planes + i, to_c * planes + (i ^ row)))
        return lax.ppermute(array, ("cells", "snap"), pairs)

    def swap(array):
        return lax.ppermute(array, "cells", [(c, c ^ 1) for c in range(devices)])

    def coded(slots):
        return ((slots * columns + tail(slots, columns), half), jnp.int16)

    def floats(*slots):
        return ((*slots, columns, half), F32)

    out2, out1, out3 = rows_of(snapshots, 2), rows_of(snapshots, 1), rows_of(snapshots, 3)
    s3 = to_plane(out3, 3)
    diagonal, weighted, square, square_other = call(
        functools.partial(early_kernel, scale),
        [((planes, rows, rows), BF16), (snapshots.shape, BF16), floats(), floats()],
        "early",
        block_offsets,
        mass_blocks,
        snapshots,
        smem=(0,),
        scratch=[pltpu.SMEM((mass_blocks.shape[0],), jnp.int32)],
    )
    s1 = to_plane(out1, 1)
    s1b = to_plane(out3, 1)
    square_arrived = swap(square_other)
    out2, weighted = lax.optimization_barrier((out2, weighted))
    s2 = to_plane(out2, 2)

    stage_c, w1 = [floats(4), coded(4)], ((components * rows, columns), BF16)
    own, other, w1 = call(
        functools.partial(stage_c_kernel, scale),
        [*stage_c, w1],
        "stage_c",
        snapshots,
        weighted,
        diagonal,
        s1,
        s3,
    )
    total, *out = call(
        combine_kernel,
        [floats(1), coded(1), coded(1), coded(1)],
        "combine_c",
        own,
        swap(other),
        scratch=[pltpu.VMEM(own.shape, F32)],
    )
    arrived = [send(out[m - 1], m, 0, (0, 1, 2, 3)) for m in (1, 2, 3)]
    sum_c, early = call(plane_c_kernel, [floats(1), coded(1)], "plane_c", total, *arrived)
    from3 = reach(early, GO_EARLY)
    s1b, s2, sum_c = lax.optimization_barrier((s1b, s2, sum_c))

    own, other = call(
        functools.partial(stage_d_kernel, scale),
        [floats(6), coded(6)],
        "stage_d",
        snapshots,
        weighted,
        diagonal,
        s1,
        w1,
        s1b,
        s2,
    )
    total, *out = call(
        combine_d_kernel,
        [floats(2), coded(2), coded(2), coded(2)],
        "combine_d",
        own,
        swap(other),
        square,
        square_arrived,
        scratch=[pltpu.VMEM(own.shape, F32)],
    )
    arrived = [send(out[m - 1], m, 0, (0, 1, 2, 3)) for m in (1, 2, 3)]
    keep, first, last = call(
        plane_d_kernel, [floats(), coded(1), coded(1)], "plane_d", total, *arrived, sum_c
    )
    arrived = [reach(first, GO_FIRST), reach(last, GO_LAST), from3]
    return call(last_kernel, [floats()], "last", keep, *arrived)[0]


def solution(mesh):
    fits = mesh.shape["cells"] == 8 and mesh.shape["snap"] == 4
    placed = (P(None, "cells", "snap"), P("cells", None, None), P("cells"))
    return jax.shard_map(
        fast if fits else general,
        mesh=mesh,
        in_specs=placed,
        out_specs=P("snap", "cells"),
        check_vma=False,
    )
```

```python
import functools

import jax
import jax.numpy as jnp
from jax import lax
from jax.experimental import pallas as pl
from jax.experimental.pallas import tpu as pltpu
from jax.sharding import PartitionSpec as P

BF16, F32 = jnp.bfloat16, jnp.float32


def general(snapshots, mass_blocks, block_offsets):
    components, cell_rows, columns_dev = snapshots.shape
    blocks_dev = mass_blocks.shape[0]
    block_size = mass_blocks.shape[1]
    base_block = lax.axis_index("cells") * blocks_dev
    local_index = block_offsets // block_size - base_block
    selected = jnp.take(
        snapshots.reshape(components, blocks_dev, block_size, columns_dev), local_index, axis=1
    )
    weighted = jnp.einsum(
        "bij,cbjs->cbis", mass_blocks, selected, preferred_element_type=F32
    ).astype(BF16)
    left_rows = selected.reshape(components * cell_rows, columns_dev)
    right_rows = weighted.reshape(components * cell_rows, columns_dev)
    product = lax.dot_general(
        left_rows,
        lax.all_gather(right_rows, "snap", axis=1, tiled=True),
        (((0,), (0,)), ((), ())),
        preferred_element_type=F32,
    )
    factor = 1.0 / float(3 * cell_rows * lax.axis_size("cells"))
    result = lax.psum_scatter(product, "cells", scatter_dimension=1, tiled=True)
    return result * factor


STAGE_C = ((1, 3), (3, 0), (3, 1), (0, 3))
STAGE_D = ((2, 0), (1, 0), (0, 2), (2, 1))
STAGE_B = ((0, 1), (1, 2))
GO_EARLY = {1: (3, 0), 2: (3, 1)}
GO_FIRST = {0: (2, 0), 1: (1, 0), 3: (2, 1)}
GO_LAST = {0: (1, 3), 2: (1, 2)}


def tdot(left, right):
    return lax.dot_general(left, right, (((0,), (0,)), ((), ())), preferred_element_type=F32)


def weigh(diagonal, piece):
    return jnp.concatenate(
        [
            jnp.dot(diagonal, piece[c], preferred_element_type=F32).astype(BF16)
            for c in range(piece.shape[0])
        ],
        axis=0,
    )


def flat(piece):
    return piece.reshape(piece.shape[0] * piece.shape[1], piece.shape[2])


def halves(core, block):
    half = block.shape[1] // 2
    low, high = block[:, :half], block[:, half:]
    first = core == 0
    return jnp.where(first, low, high), jnp.where(first, high, low)


def early_kernel(
    scale, offsets_ref, mass_ref, s_ref, diagonal_ref, weighted_ref, own_ref, other_ref, where_ref
):
    components = s_ref.shape[0]
    blocks, size, _ = mass_ref.shape
    quarters, rows, _ = diagonal_ref.shape
    cells = lax.axis_index("cells")
    base = cells * blocks
    for b in range(blocks):
        where_ref[offsets_ref[b] // size - base] = b
    diagonal_ref[...] = jnp.zeros_like(diagonal_ref)
    per = blocks // quarters
    for t in range(quarters):
        for i in range(per):
            diagonal_ref[t, i * size : (i + 1) * size, i * size : (i + 1) * size] = mass_ref[
                where_ref[t * per + i]
            ]
    for t in range(quarters):
        for c in range(components):
            rows_now = slice(t * rows, (t + 1) * rows)
            weighted_ref[c, rows_now, :] = jnp.dot(
                diagonal_ref[t], s_ref[c, rows_now, :], preferred_element_type=F32
            ).astype(BF16)
    total = tdot(s_ref[0], weighted_ref[0])
    for c in range(1, components):
        total += tdot(s_ref[c], weighted_ref[c])
    own_ref[...], other_ref[...] = halves(cells % 2, total * scale)


def emit(scale, blocks, own_ref, other_ref):
    core = lax.axis_index("cells") % 2
    others = []
    for at, block in enumerate(blocks):
        own_ref[at], other = halves(core, block * scale)
        others.append(other)
    encode(jnp.stack(others), other_ref)


def quarter(z, ref):
    rows = ref.shape[1] // lax.axis_size("snap")
    return flat(ref[:, pl.ds(pl.multiple_of(z * rows, rows), rows), :])


def stage_c_kernel(
    scale,
    s_ref,
    weighted_ref,
    diagonal_ref,
    s1_ref,
    s3_ref,
    own_ref,
    other_ref,
    w1_ref,
    left_ref,
    pair_ref,
):
    z = lax.axis_index("snap")
    diagonal = diagonal_ref[z]
    s0, w0 = quarter(z, s_ref), quarter(z, weighted_ref)
    s1, s3 = flat(s1_ref[...]), flat(s3_ref[...])
    w1, w3 = weigh(diagonal, s1_ref[...]), weigh(diagonal, s3_ref[...])
    s0t, s1t = s0.T, s1.T
    blocks = {
        (3, 0): tdot(s3, w0),
        (3, 1): tdot(s3, w1),
        (0, 3): jnp.dot(s0t, w3, preferred_element_type=F32),
        (1, 3): jnp.dot(s1t, w3, preferred_element_type=F32),
    }
    emit(scale, [blocks[name] for name in STAGE_C], own_ref, other_ref)
    w1_ref[...] = w1
    left_ref[0], left_ref[1] = s0t, s1t
    pair_ref[0] = jnp.dot(s0t, w1, preferred_element_type=F32)
    pair_ref[1] = jnp.dot(s1t, w0, preferred_element_type=F32)


def stage_d_kernel(
    scale,
    s_ref,
    weighted_ref,
    diagonal_ref,
    left_ref,
    pair_ref,
    w1_ref,
    s1b_ref,
    s2_ref,
    own_ref,
    other_ref,
):
    z = lax.axis_index("snap")
    across = z ^ 2
    w0, w1 = quarter(z, weighted_ref), w1_ref[...]
    s0b, w0b = quarter(across, s_ref), quarter(across, weighted_ref)
    s1b, s2 = flat(s1b_ref[...]), flat(s2_ref[...])
    w1b = weigh(diagonal_ref[across], s1b_ref[...])
    w2 = weigh(diagonal_ref[z], s2_ref[...])
    blocks = {
        (0, 1): pair_ref[0] + tdot(s0b, w1b),
        (1, 0): pair_ref[1] + tdot(s1b, w0b),
        (2, 0): tdot(s2, w0),
        (2, 1): tdot(s2, w1),
        (0, 2): jnp.dot(left_ref[0], w2, preferred_element_type=F32),
        (1, 2): jnp.dot(left_ref[1], w2, preferred_element_type=F32),
    }
    emit(scale, [blocks[name] for name in STAGE_D + STAGE_B], own_ref, other_ref)


GROUP = 64
STEPS = 256.0
TOP = 32700.0
LEAST = 1e-33


def tail(slots, rows):
    return -(-slots * rows // (GROUP * 16)) * 16


def encode(value, message_ref):
    slots, rows, columns = value.shape
    groups = slots * rows // GROUP
    value = value.reshape(groups, GROUP, columns)
    most = jnp.maximum(jnp.max(jnp.abs(value), axis=1), LEAST)
    step = jnp.ceil(jnp.log2(most) * STEPS)
    code = jnp.round(value * (TOP * jnp.exp2(step * (-1.0 / STEPS)))[:, None, :])
    codes = code.reshape(slots * rows, columns).astype(jnp.int32).astype(jnp.int16)
    message_ref[: slots * rows] = codes
    more = tail(slots, rows) - groups
    if more:
        step = jnp.concatenate([step, jnp.zeros((more, columns), F32)], axis=0)
    message_ref[slots * rows :] = step.astype(jnp.int32).astype(jnp.int16)


def decode(message_ref, slots, rows):
    columns = message_ref.shape[1]
    groups = slots * rows // GROUP
    step = message_ref[slots * rows :].astype(jnp.int32).astype(F32)[:groups]
    code = message_ref[: slots * rows].astype(jnp.int32).astype(F32)
    value = code.reshape(groups, GROUP, columns) * (jnp.exp2(step * (1.0 / STEPS)) * (1.0 / TOP))[:, None, :]
    return value.reshape(slots, rows, columns)


def place():
    return (lax.axis_index("cells") // 2) ^ lax.axis_index("snap")


def combine_kernel(own_ref, arrived_ref, total_ref, *refs):
    *message_refs, whole_ref = refs
    q = place()
    whole_ref[...] = own_ref[...] + decode(arrived_ref, *own_ref.shape[:2])
    total_ref[...] = whole_ref[pl.ds(q, 1)]
    for m, ref in enumerate(message_refs, 1):
        encode(whole_ref[pl.ds(q ^ m, 1)], ref)


def combine_d_kernel(own_ref, arrived_ref, square_ref, other_ref, total_ref, *refs):
    *message_refs, whole_ref = refs
    q = place()
    whole_ref[...] = own_ref[...] + decode(arrived_ref, *own_ref.shape[:2])
    square = square_ref[...] + other_ref[...]
    for m, ref in enumerate((total_ref, *message_refs)):
        to = q ^ m
        second = jnp.where(to == 0, square, jnp.where(to == 1, whole_ref[4], whole_ref[5]))
        value = jnp.stack([whole_ref[to], second])
        if m == 0:
            ref[...] = value
        else:
            encode(value, ref)


def plane_sum(total_ref, message_refs):
    total = total_ref[...]
    for ref in message_refs:
        total += decode(ref, *total.shape[:2])
    return total


def plane_c_kernel(total_ref, m1_ref, m2_ref, m3_ref, sum_ref, three_ref):
    total = plane_sum(total_ref, (m1_ref, m2_ref, m3_ref))
    sum_ref[...] = total
    encode(total, three_ref)


def plane_d_kernel(total_ref, m1_ref, m2_ref, m3_ref, sum_c_ref, keep_ref, first_ref, last_ref):
    q = place()
    total = plane_sum(total_ref, (m1_ref, m2_ref, m3_ref))
    sum_c = sum_c_ref[...]
    encode(total[:1], first_ref)
    encode(jnp.where(q == 0, sum_c, total[1:]), last_ref)
    keep_ref[...] = jnp.where(q < 2, total[1], jnp.where(q == 3, sum_c[0], total[0]))


def last_kernel(keep_ref, m1_ref, m2_ref, m3_ref, out_ref):
    total = keep_ref[...]
    for ref in (m1_ref, m2_ref, m3_ref):
        total += decode(ref, 1, total.shape[0])[0]
    out_ref[...] = total


def call(kernel, outs, name, *args, smem=(), scratch=()):
    vmem, scalar = pl.BlockSpec(memory_space=pltpu.VMEM), pl.BlockSpec(memory_space=pltpu.SMEM)
    return pl.pallas_call(
        kernel,
        out_shape=[jax.ShapeDtypeStruct(s, t) for s, t in outs],
        in_specs=[scalar if k in smem else vmem for k in range(len(args))],
        out_specs=[vmem] * len(outs),
        scratch_shapes=scratch,
        compiler_params=pltpu.CompilerParams(vmem_limit_bytes=LIMIT),
        cost_estimate=pl.CostEstimate(flops=0, bytes_accessed=0, transcendentals=0),
        name=name,
    )(*args)


LIMIT = 24 * 2**20


def fast(snapshots, mass_blocks, block_offsets):
    components, cell_rows, columns = snapshots.shape
    planes, devices = lax.axis_size("snap"), lax.axis_size("cells")
    rows, half = cell_rows // planes, columns // 2
    scale = 1.0 / float(components * cell_rows * devices)
    z = lax.axis_index("snap")

    def to_plane(array, m):
        return lax.ppermute(array, "snap", [(i, i ^ m) for i in range(planes)])

    def rows_of(array, m):
        return lax.dynamic_slice_in_dim(array, (z ^ m) * rows, rows, axis=1)

    def send(array, m, k, wanted):
        pairs = []
        for c in range(devices):
            for i in range(planes):
                to_c, to_i = c ^ (2 * m), i ^ k
                if ((to_c // 2) ^ to_i) in wanted:
                    pairs.append((c * planes + i, to_c * planes + to_i))
        return lax.ppermute(array, ("cells", "snap"), pairs)

    def reach(array, blocks):
        pairs = []
        for c in range(devices):
            for i in range(planes):
                if (c // 2) ^ i in blocks:
                    row, column = blocks[(c // 2) ^ i]
                    to_c = 2 * (i ^ column) + c % 2
                    pairs.append((c * planes + i, to_c * planes + (i ^ row)))
        return lax.ppermute(array, ("cells", "snap"), pairs)

    def swap(array):
        return lax.ppermute(array, "cells", [(c, c ^ 1) for c in range(devices)])

    def coded(slots):
        return ((slots * columns + tail(slots, columns), half), jnp.int16)

    def floats(*slots):
        return ((*slots, columns, half), F32)

    out2, out1, out3 = rows_of(snapshots, 2), rows_of(snapshots, 1), rows_of(snapshots, 3)
    s3 = to_plane(out3, 3)
    diagonal, weighted, square, square_other = call(
        functools.partial(early_kernel, scale),
        [((planes, rows, rows), BF16), (snapshots.shape, BF16), floats(), floats()],
        "early",
        block_offsets,
        mass_blocks,
        snapshots,
        smem=(0,),
        scratch=[pltpu.SMEM((mass_blocks.shape[0],), jnp.int32)],
    )
    s1 = to_plane(out1, 1)
    s1b = to_plane(out3, 1)
    square_arrived = swap(square_other)
    out2, square_arrived = lax.optimization_barrier((out2, square_arrived))
    s2 = to_plane(out2, 2)

    held = components * rows
    own, other, w1, left, pair = call(
        functools.partial(stage_c_kernel, scale),
        [
            floats(4),
            coded(4),
            ((held, columns), BF16),
            ((2, columns, held), BF16),
            ((2, columns, columns), F32),
        ],
        "stage_c",
        snapshots,
        weighted,
        diagonal,
        s1,
        s3,
    )
    total, *out = call(
        combine_kernel,
        [floats(1), coded(1), coded(1), coded(1)],
        "combine_c",
        own,
        swap(other),
        scratch=[pltpu.VMEM(own.shape, F32)],
    )
    arrived = [send(out[m - 1], m, 0, (0, 1, 2, 3)) for m in (1, 2, 3)]
    sum_c, early = call(plane_c_kernel, [floats(1), coded(1)], "plane_c", total, *arrived)
    from3 = reach(early, GO_EARLY)
    s1b, s2, sum_c = lax.optimization_barrier((s1b, s2, sum_c))

    own, other = call(
        functools.partial(stage_d_kernel, scale),
        [floats(6), coded(6)],
        "stage_d",
        snapshots,
        weighted,
        diagonal,
        left,
        pair,
        w1,
        s1b,
        s2,
    )
    total, *out = call(
        combine_d_kernel,
        [floats(2), coded(2), coded(2), coded(2)],
        "combine_d",
        own,
        swap(other),
        square,
        square_arrived,
        scratch=[pltpu.VMEM(own.shape, F32)],
    )
    arrived = [send(out[m - 1], m, 0, (0, 1, 2, 3)) for m in (1, 2, 3)]
    keep, first, last = call(
        plane_d_kernel, [floats(), coded(1), coded(1)], "plane_d", total, *arrived, sum_c
    )
    arrived = [reach(first, GO_FIRST), reach(last, GO_LAST), from3]
    return call(last_kernel, [floats()], "last", keep, *arrived)[0]


def solution(mesh):
    fits = mesh.shape["cells"] == 8 and mesh.shape["snap"] == 4
    placed = (P(None, "cells", "snap"), P("cells", None, None), P("cells"))
    return jax.shard_map(
        fast if fits else general,
        mesh=mesh,
        in_specs=placed,
        out_specs=P("snap", "cells"),
        check_vma=False,
    )
```

```python
import functools

import jax
import jax.numpy as jnp
from jax import lax
from jax.experimental import pallas as pl
from jax.experimental.pallas import tpu as pltpu
from jax.sharding import PartitionSpec as P

BF16, F32 = jnp.bfloat16, jnp.float32


def general(snapshots, mass_blocks, block_offsets):
    components, cell_rows, columns_dev = snapshots.shape
    blocks_dev = mass_blocks.shape[0]
    block_size = mass_blocks.shape[1]
    base_block = lax.axis_index("cells") * blocks_dev
    local_index = block_offsets // block_size - base_block
    selected = jnp.take(
        snapshots.reshape(components, blocks_dev, block_size, columns_dev), local_index, axis=1
    )
    weighted = jnp.einsum(
        "bij,cbjs->cbis", mass_blocks, selected, preferred_element_type=F32
    ).astype(BF16)
    left_rows = selected.reshape(components * cell_rows, columns_dev)
    right_rows = weighted.reshape(components * cell_rows, columns_dev)
    product = lax.dot_general(
        left_rows,
        lax.all_gather(right_rows, "snap", axis=1, tiled=True),
        (((0,), (0,)), ((), ())),
        preferred_element_type=F32,
    )
    factor = 1.0 / float(3 * cell_rows * lax.axis_size("cells"))
    result = lax.psum_scatter(product, "cells", scatter_dimension=1, tiled=True)
    return result * factor


STAGE_C = ((1, 3), (3, 0), (3, 1), (0, 3))
STAGE_D = ((2, 0), (2, 1), (0, 2), (1, 0))
STAGE_B = ((0, 1), (1, 2))
GO_EARLY = {1: (3, 0), 2: (3, 1)}
GO_FIRST = {0: (2, 0), 1: (2, 1), 3: (1, 0)}
GO_NEXT = {0: (1, 3)}
GO_LAST = {2: (1, 2)}


def tdot(left, right):
    return lax.dot_general(left, right, (((0,), (0,)), ((), ())), preferred_element_type=F32)


def weigh(diagonal, piece):
    return jnp.concatenate(
        [
            jnp.dot(diagonal, piece[c], preferred_element_type=F32).astype(BF16)
            for c in range(piece.shape[0])
        ],
        axis=0,
    )


def flat(piece):
    return piece.reshape(piece.shape[0] * piece.shape[1], piece.shape[2])


def halves(core, block):
    half = block.shape[1] // 2
    low, high = block[:, :half], block[:, half:]
    first = core == 0
    return jnp.where(first, low, high), jnp.where(first, high, low)


def early_kernel(
    scale, offsets_ref, mass_ref, s_ref, diagonal_ref, weighted_ref, own_ref, other_ref, where_ref
):
    components = s_ref.shape[0]
    blocks, size, _ = mass_ref.shape
    quarters, rows, _ = diagonal_ref.shape
    cells = lax.axis_index("cells")
    base = cells * blocks
    for b in range(blocks):
        where_ref[offsets_ref[b] // size - base] = b
    diagonal_ref[...] = jnp.zeros_like(diagonal_ref)
    per = blocks // quarters
    for t in range(quarters):
        for i in range(per):
            diagonal_ref[t, i * size : (i + 1) * size, i * size : (i + 1) * size] = mass_ref[
                where_ref[t * per + i]
            ]
    for t in range(quarters):
        for c in range(components):
            rows_now = slice(t * rows, (t + 1) * rows)
            weighted_ref[c, rows_now, :] = jnp.dot(
                diagonal_ref[t], s_ref[c, rows_now, :], preferred_element_type=F32
            ).astype(BF16)
    total = tdot(s_ref[0], weighted_ref[0])
    for c in range(1, components):
        total += tdot(s_ref[c], weighted_ref[c])
    own_ref[...], other_ref[...] = halves(cells % 2, total * scale)


def emit(scale, blocks, own_ref, other_ref):
    core = lax.axis_index("cells") % 2
    others = []
    for at, block in enumerate(blocks):
        own_ref[at], other = halves(core, block * scale)
        others.append(other)
    encode(jnp.stack(others), other_ref)


def quarter(z, ref):
    rows = ref.shape[1] // lax.axis_size("snap")
    return flat(ref[:, pl.ds(pl.multiple_of(z * rows, rows), rows), :])


def stage_c_kernel(
    scale,
    s_ref,
    weighted_ref,
    diagonal_ref,
    s1_ref,
    s3_ref,
    own_ref,
    other_ref,
    w1_ref,
    left_ref,
    pair_ref,
):
    z = lax.axis_index("snap")
    diagonal = diagonal_ref[z]
    s0, w0 = quarter(z, s_ref), quarter(z, weighted_ref)
    s1, s3 = flat(s1_ref[...]), flat(s3_ref[...])
    w1, w3 = weigh(diagonal, s1_ref[...]), weigh(diagonal, s3_ref[...])
    s0t, s1t = s0.T, s1.T
    blocks = {
        (3, 0): tdot(s3, w0),
        (3, 1): tdot(s3, w1),
        (0, 3): jnp.dot(s0t, w3, preferred_element_type=F32),
        (1, 3): jnp.dot(s1t, w3, preferred_element_type=F32),
    }
    emit(scale, [blocks[name] for name in STAGE_C], own_ref, other_ref)
    w1_ref[...] = w1
    left_ref[0], left_ref[1] = s0t, s1t
    pair_ref[0] = jnp.dot(s0t, w1, preferred_element_type=F32)
    pair_ref[1] = jnp.dot(s1t, w0, preferred_element_type=F32)


def stage_d_kernel(
    scale,
    s_ref,
    weighted_ref,
    diagonal_ref,
    left_ref,
    pair_ref,
    w1_ref,
    s1b_ref,
    s2_ref,
    own_ref,
    other_ref,
):
    z = lax.axis_index("snap")
    across = z ^ 2
    w0, w1 = quarter(z, weighted_ref), w1_ref[...]
    s0b, w0b = quarter(across, s_ref), quarter(across, weighted_ref)
    s1b, s2 = flat(s1b_ref[...]), flat(s2_ref[...])
    w1b = weigh(diagonal_ref[across], s1b_ref[...])
    w2 = weigh(diagonal_ref[z], s2_ref[...])
    blocks = {
        (0, 1): pair_ref[0] + tdot(s0b, w1b),
        (1, 0): pair_ref[1] + tdot(s1b, w0b),
        (2, 0): tdot(s2, w0),
        (2, 1): tdot(s2, w1),
        (0, 2): jnp.dot(left_ref[0], w2, preferred_element_type=F32),
        (1, 2): jnp.dot(left_ref[1], w2, preferred_element_type=F32),
    }
    emit(scale, [blocks[name] for name in STAGE_D + STAGE_B], own_ref, other_ref)


GROUP = 128
STEPS = 256.0
TOP = 32700.0
LEAST = 1e-33


def tail(slots, rows):
    return -(-slots * rows // (GROUP * 16)) * 16


def encode(value, message_ref):
    slots, rows, columns = value.shape
    groups = slots * rows // GROUP
    value = value.reshape(groups, GROUP, columns)
    most = jnp.maximum(jnp.max(jnp.abs(value), axis=1), LEAST)
    step = jnp.ceil(jnp.log2(most) * STEPS)
    code = jnp.round(value * (TOP * jnp.exp2(step * (-1.0 / STEPS)))[:, None, :])
    codes = code.reshape(slots * rows, columns).astype(jnp.int32).astype(jnp.int16)
    message_ref[: slots * rows] = codes
    more = tail(slots, rows) - groups
    if more:
        step = jnp.concatenate([step, jnp.zeros((more, columns), F32)], axis=0)
    message_ref[slots * rows :] = step.astype(jnp.int32).astype(jnp.int16)


def decode(message_ref, slots, rows):
    columns = message_ref.shape[1]
    groups = slots * rows // GROUP
    step = message_ref[slots * rows :].astype(jnp.int32).astype(F32)[:groups]
    code = message_ref[: slots * rows].astype(jnp.int32).astype(F32)
    value = code.reshape(groups, GROUP, columns) * (jnp.exp2(step * (1.0 / STEPS)) * (1.0 / TOP))[:, None, :]
    return value.reshape(slots, rows, columns)


def place():
    return (lax.axis_index("cells") // 2) ^ lax.axis_index("snap")


def combine_kernel(own_ref, arrived_ref, total_ref, *refs):
    *message_refs, whole_ref = refs
    q = place()
    whole_ref[...] = own_ref[...] + decode(arrived_ref, *own_ref.shape[:2])
    total_ref[...] = whole_ref[pl.ds(q, 1)]
    for m, ref in enumerate(message_refs, 1):
        encode(whole_ref[pl.ds(q ^ m, 1)], ref)


def combine_d_kernel(own_ref, arrived_ref, square_ref, other_ref, total_ref, *refs):
    *message_refs, whole_ref = refs
    q = place()
    whole_ref[...] = own_ref[...] + decode(arrived_ref, *own_ref.shape[:2])
    square = square_ref[...] + other_ref[...]
    for m, ref in enumerate((total_ref, *message_refs)):
        to = q ^ m
        second = jnp.where(to == 0, square, jnp.where(to == 1, whole_ref[4], whole_ref[5]))
        value = jnp.stack([whole_ref[to], second])
        if m == 0:
            ref[...] = value
        else:
            encode(value, ref)


def plane_sum(total_ref, message_refs):
    total = total_ref[...]
    for ref in message_refs:
        total += decode(ref, *total.shape[:2])
    return total


def plane_c_kernel(total_ref, m1_ref, m2_ref, m3_ref, sum_ref, three_ref):
    total = plane_sum(total_ref, (m1_ref, m2_ref, m3_ref))
    sum_ref[...] = total
    encode(total, three_ref)


def plane_d_kernel(total_ref, m1_ref, m2_ref, m3_ref, sum_c_ref, keep_ref, first_ref, last_ref):
    q = place()
    total = plane_sum(total_ref, (m1_ref, m2_ref, m3_ref))
    sum_c = sum_c_ref[...]
    encode(total[:1], first_ref)
    encode(total[1:], last_ref)
    keep_ref[...] = jnp.where(q < 2, total[1], jnp.where(q == 3, sum_c[0], total[0]))


def last_kernel(keep_ref, *refs):
    *message_refs, out_ref = refs
    total = keep_ref[...]
    for ref in message_refs:
        total += decode(ref, 1, total.shape[0])[0]
    out_ref[...] = total


def call(kernel, outs, name, *args, smem=(), scratch=()):
    vmem, scalar = pl.BlockSpec(memory_space=pltpu.VMEM), pl.BlockSpec(memory_space=pltpu.SMEM)
    return pl.pallas_call(
        kernel,
        out_shape=[jax.ShapeDtypeStruct(s, t) for s, t in outs],
        in_specs=[scalar if k in smem else vmem for k in range(len(args))],
        out_specs=[vmem] * len(outs),
        scratch_shapes=scratch,
        compiler_params=pltpu.CompilerParams(vmem_limit_bytes=LIMIT),
        cost_estimate=pl.CostEstimate(flops=0, bytes_accessed=0, transcendentals=0),
        name=name,
    )(*args)


LIMIT = 24 * 2**20


def fast(snapshots, mass_blocks, block_offsets):
    components, cell_rows, columns = snapshots.shape
    planes, devices = lax.axis_size("snap"), lax.axis_size("cells")
    rows, half = cell_rows // planes, columns // 2
    scale = 1.0 / float(components * cell_rows * devices)
    z = lax.axis_index("snap")

    def to_plane(array, m):
        return lax.ppermute(array, "snap", [(i, i ^ m) for i in range(planes)])

    def rows_of(array, m):
        return lax.dynamic_slice_in_dim(array, (z ^ m) * rows, rows, axis=1)

    def send(array, m, k, wanted):
        pairs = []
        for c in range(devices):
            for i in range(planes):
                to_c, to_i = c ^ (2 * m), i ^ k
                if ((to_c // 2) ^ to_i) in wanted:
                    pairs.append((c * planes + i, to_c * planes + to_i))
        return lax.ppermute(array, ("cells", "snap"), pairs)

    def reach(array, blocks):
        pairs = []
        for c in range(devices):
            for i in range(planes):
                if (c // 2) ^ i in blocks:
                    row, column = blocks[(c // 2) ^ i]
                    to_c = 2 * (i ^ column) + c % 2
                    pairs.append((c * planes + i, to_c * planes + (i ^ row)))
        return lax.ppermute(array, ("cells", "snap"), pairs)

    def swap(array):
        return lax.ppermute(array, "cells", [(c, c ^ 1) for c in range(devices)])

    def coded(slots):
        return ((slots * columns + tail(slots, columns), half), jnp.int16)

    def floats(*slots):
        return ((*slots, columns, half), F32)

    out2, out1, out3 = rows_of(snapshots, 2), rows_of(snapshots, 1), rows_of(snapshots, 3)
    s3 = to_plane(out3, 3)
    diagonal, weighted, square, square_other = call(
        functools.partial(early_kernel, scale),
        [((planes, rows, rows), BF16), (snapshots.shape, BF16), floats(), floats()],
        "early",
        block_offsets,
        mass_blocks,
        snapshots,
        smem=(0,),
        scratch=[pltpu.SMEM((mass_blocks.shape[0],), jnp.int32)],
    )
    s1 = to_plane(out1, 1)
    s1b = to_plane(out3, 1)
    square_arrived = swap(square_other)
    out2, square_arrived = lax.optimization_barrier((out2, square_arrived))
    s2 = to_plane(out2, 2)

    held = components * rows
    own, other, w1, left, pair = call(
        functools.partial(stage_c_kernel, scale),
        [
            floats(4),
            coded(4),
            ((held, columns), BF16),
            ((2, columns, held), BF16),
            ((2, columns, columns), F32),
        ],
        "stage_c",
        snapshots,
        weighted,
        diagonal,
        s1,
        s3,
    )
    total, *out = call(
        combine_kernel,
        [floats(1), coded(1), coded(1), coded(1)],
        "combine_c",
        own,
        swap(other),
        scratch=[pltpu.VMEM(own.shape, F32)],
    )
    arrived = [send(out[m - 1], m, 0, (0, 1, 2, 3)) for m in (1, 2, 3)]
    sum_c, early = call(plane_c_kernel, [floats(1), coded(1)], "plane_c", total, *arrived)
    from3 = reach(early, GO_EARLY)
    from1 = reach(early, GO_NEXT)
    s1b, s2, sum_c = lax.optimization_barrier((s1b, s2, sum_c))

    own, other = call(
        functools.partial(stage_d_kernel, scale),
        [floats(6), coded(6)],
        "stage_d",
        snapshots,
        weighted,
        diagonal,
        left,
        pair,
        w1,
        s1b,
        s2,
    )
    total, *out = call(
        combine_d_kernel,
        [floats(2), coded(2), coded(2), coded(2)],
        "combine_d",
        own,
        swap(other),
        square,
        square_arrived,
        scratch=[pltpu.VMEM(own.shape, F32)],
    )
    arrived = [send(out[m - 1], m, 0, (0, 1, 2, 3)) for m in (1, 2, 3)]
    keep, first, last = call(
        plane_d_kernel, [floats(), coded(1), coded(1)], "plane_d", total, *arrived, sum_c
    )
    arrived = [reach(first, GO_FIRST), reach(last, GO_LAST), from3, from1]
    return call(last_kernel, [floats()], "last", keep, *arrived)[0]


def solution(mesh):
    fits = mesh.shape["cells"] == 8 and mesh.shape["snap"] == 4
    placed = (P(None, "cells", "snap"), P("cells", None, None), P("cells"))
    return jax.shard_map(
        fast if fits else general,
        mesh=mesh,
        in_specs=placed,
        out_specs=P("snap", "cells"),
        check_vma=False,
    )
```
